512 devices in a mesh: pool: 64 (over y, z), ctx: 8 (over x, core).
Axes of the slice: x: 4, y: 4, z: 16, core: 2. Of those that a mesh axis runs over, the one named last changes fastest.
Arguments:
- fresh_q: bfloat16 [4096, 8192], P('pool', 'ctx'), may hold values from -180 to 180
- fresh_kv: bfloat16 [4096, 2048], P('pool', 'ctx'), may hold values from -6 to 6
- pool_kv: bfloat16 [256, 512, 2048], P(None, 'pool', 'ctx'), may hold values from -6 to 6
- passage_lists: int32 [4, 32], replicated, may hold values from 0 to 255
- slot_map: int32 [256], replicated, may hold values from 0 to 255, each once
- rec_pos: int32 [64, 64], P('pool'), may hold values from 0 to 1023, as said below
Outputs:
- attn_out: bfloat16 [4096, 8192], P('pool', 'ctx')
- deviation: float32 [4096], P('pool')
The draws below stay inside these ranges and needn't reach their ends.
Inputs may be any that keep to these rules, and one draw needn't show every extreme that they name: `rec_pos`: the 64 offsets of one tile are distinct. `slot_map`: each passage has a row of its own in the store.
All inputs are finite; a program needn't handle non-finite values.
Results may differ from the reference program's by a relative error of at most 0.017.
Values may be sent and summed in bfloat16 or wider, within the bound.
A program may use at most 64 MiB of HBM per device.

```python
import math
import jax
import jax.numpy as jnp
import numpy as np
from jax import lax

HEADS = 64
KVH = 8
HD = 128
PASSAGE = 512
BLOCK_PASSAGES = 2
SEQ_BLOCKS = 16
ROWS = 64
REQS = 4
TILES = 64
NCHUNK = 256


def draw_fresh_q(key, part):
    key = jax.random.fold_in(key, 5)
    base_key = jax.random.fold_in(key, 0)
    shape_all = (TILES * ROWS, HEADS * HD)
    drawn = 2.5 * jax.random.truncated_normal(base_key, -6.0, 6.0, shape_all, jnp.float32)
    return drawn.astype(jnp.bfloat16)


def draw_rec_pos(key, part):
    key = jax.random.fold_in(key, 11)
    tile_keys = jax.random.split(key, TILES)

    def one_tile(tile_key):
        return jax.random.permutation(tile_key, BLOCK_PASSAGES * PASSAGE)[:ROWS].astype(jnp.int32)
    return jax.vmap(one_tile)(tile_keys)


def with_ends(result, rng, low, largest):
    longest = result.shape.index(max(result.shape))
    spots = []
    for shift in (0, 1):
        where = [jax.random.randint(jax.random.fold_in(rng, axis), (), 0, length) for axis, length in enumerate(result.shape)]
        where[longest] = (where[longest] + shift) % result.shape[longest]
        spots.append(tuple(where))
    return result.at[spots[0]].set(low).at[spots[1]].set(largest)


def levels(own_key, shape, cuts, least, high):
    gain, own = 1.0, jax.random.fold_in(own_key, 6)
    for position, shards_of in cuts:
        draws = jnp.exp(jax.random.uniform(jax.random.fold_in(own, position), (shards_of,), jnp.float32, least / len(cuts), high / len(cuts)))
        gain = gain * jnp.repeat(draws, shape[position] // shards_of).reshape([-1 if axis == position else 1 for axis in range(len(shape))])
    return gain


def rank_table(amount, skew):
    portions = [(1 << 20) // math.isqrt(standing ** skew) + 1 for standing in range(1, amount + 1)]
    scale = 1 + sum(portions) // (1 << 30)
    return np.cumsum(np.array([max(1, weight // scale) for weight in portions]))


def ranked_ids(stream_key, extent, amount, skew):
    listing = rank_table(amount, skew)
    ticket = jax.random.randint(jax.random.fold_in(stream_key, 1), extent, 0, int(listing[amount - 1]))
    standing = jnp.searchsorted(jnp.asarray(listing, jnp.int32), ticket, side="right")
    return jax.random.permutation(jax.random.fold_in(stream_key, 2), amount)[standing].astype(jnp.int32)


def scatter_about(rng, extent, width, reach, pieces=(), kind=jnp.bfloat16):
    result = width * jax.random.normal(rng, extent, jnp.float32)
    if pieces:
        result = result * levels(rng, extent, pieces, -0.22, 0.18)
    return jnp.clip(result, -reach, reach).astype(kind)


def setup_inputs(seed: int = 0) -> dict:
    key_list = jax.random.split(jax.random.key(seed), 7)
    fresh_q = draw_fresh_q(jax.random.fold_in(key_list[6], 71), 0)
    fresh_kv = scatter_about(key_list[1], (TILES * ROWS, KVH * 2 * HD), 1.0, 6.0, ((0, 64), (1, 8)))
    pool_kv = scatter_about(key_list[2], (NCHUNK, PASSAGE, KVH * 2 * HD), 1.0, 6.0, ((1, 64), (2, 8)))
    passage_lists = with_ends(ranked_ids(key_list[3], (REQS, SEQ_BLOCKS * BLOCK_PASSAGES), NCHUNK, 2), jax.random.fold_in(key_list[3], 3), 0, NCHUNK - 1).astype(jnp.int32)
    slot_map = jax.random.permutation(key_list[4], NCHUNK).astype(jnp.int32)
    rec_pos = draw_rec_pos(jax.random.fold_in(key_list[6], 71), 0)
    return {"fresh_q": fresh_q, "fresh_kv": fresh_kv, "pool_kv": pool_kv, "passage_lists": passage_lists, "slot_map": slot_map, "rec_pos": rec_pos}


rope_base = 500000.0

def rope_angles(positions, head_dim):
    half_dim = head_dim // 2
    frequency = jnp.exp(jnp.arange(half_dim, dtype=jnp.float32) * (-2.0 * math.log(rope_base) / head_dim))
    angles = positions.astype(jnp.float32)[..., None] * frequency
    return (jnp.cos(angles), jnp.sin(angles))

def rotate(vectors, cosine, sine_part):
    half_dim = vectors.shape[-1] // 2
    former = vectors[..., :half_dim]
    latter = vectors[..., half_dim:]
    return jnp.concatenate([former * cosine - latter * sine_part, latter * cosine + former * sine_part], axis=-1)

def reference(fresh_q, fresh_kv, pool_kv, passage_lists, slot_map, rec_pos):
    block_span = BLOCK_PASSAGES * PASSAGE
    seq_len = SEQ_BLOCKS * block_span
    passage_total = SEQ_BLOCKS * BLOCK_PASSAGES
    request_rows = SEQ_BLOCKS * ROWS
    group_size = HEADS // KVH
    score_scale = 1.0 / math.sqrt(HD)

    def one_request(request):
        passage_slots = jnp.take(slot_map, jnp.take(passage_lists, request, axis=0))
        page_rows = jnp.take(pool_kv, passage_slots, axis=0).reshape(passage_total, PASSAGE, KVH, 2, HD)
        offsets = jnp.arange(passage_total, dtype=jnp.int32) * PASSAGE
        cosine, sine_part = rope_angles(offsets, HD)
        cached_keys = rotate(page_rows[:, :, :, 0].astype(jnp.float32), cosine[:, None, None, :], sine_part[:, None, None, :])
        cached_keys = cached_keys.astype(jnp.bfloat16).reshape(seq_len, KVH, HD)
        cached_values = page_rows[:, :, :, 1].reshape(seq_len, KVH, HD)
        tile_pos = lax.dynamic_slice_in_dim(rec_pos, (request * SEQ_BLOCKS).astype(jnp.int32), SEQ_BLOCKS, 0)
        block_starts = jnp.arange(SEQ_BLOCKS, dtype=jnp.int32) * block_span
        positions = (tile_pos + block_starts[:, None]).reshape(request_rows).astype(jnp.int32)
        first_row = (request * request_rows).astype(jnp.int32)
        query_rows = lax.dynamic_slice_in_dim(fresh_q, first_row, request_rows, 0).reshape(request_rows, HEADS, HD)
        fresh_rows = lax.dynamic_slice_in_dim(fresh_kv, first_row, request_rows, 0).reshape(request_rows, KVH, 2, HD)
        cos_rows, sin_rows = rope_angles(positions, HD)
        queries = rotate(query_rows.astype(jnp.float32), cos_rows[:, None, :], sin_rows[:, None, :]).astype(jnp.bfloat16)
        fresh_keys = rotate(fresh_rows[:, :, 0].astype(jnp.float32), cos_rows[:, None, :], sin_rows[:, None, :]).astype(jnp.bfloat16)
        cached_here = jnp.take(cached_keys, positions, axis=0)
        gap_vals = cached_here.astype(jnp.float32) - fresh_keys.astype(jnp.float32)
        deviation = lax.optimization_barrier(jnp.sum(gap_vals * gap_vals, axis=(1, 2))) / (KVH * HD)
        key_rows = cached_keys.at[positions].set(fresh_keys)
        value_rows = cached_values.at[positions].set(fresh_rows[:, :, 1])
        allowed = jnp.arange(seq_len, dtype=jnp.int32)[None, :] <= positions[:, None]

        def one_head(head):
            head_queries = jnp.take(queries, head, axis=1)
            head_keys = jnp.take(key_rows, head // group_size, axis=1)
            head_values = jnp.take(value_rows, head // group_size, axis=1)
            scores = jnp.dot(head_queries, head_keys.T, preferred_element_type=jnp.float32) * score_scale
            scores = jnp.where(allowed, scores, -jnp.inf)
            weights = jnp.exp(scores - lax.optimization_barrier(jnp.max(scores, axis=1, keepdims=True)))
            totals = lax.optimization_barrier(jnp.sum(weights, axis=1, keepdims=True))
            return jnp.dot(weights.astype(jnp.bfloat16), head_values, preferred_element_type=jnp.float32) / totals
        per_head = lax.map(one_head, jnp.arange(HEADS, dtype=jnp.int32))
        attended = per_head.transpose(1, 0, 2).reshape(request_rows, HEADS * HD).astype(jnp.bfloat16)
        return (attended, deviation)
    attended, deviation = lax.map(one_request, jnp.arange(REQS, dtype=jnp.int32))
    return (attended.reshape(REQS * request_rows, HEADS * HD), deviation.reshape(REQS * request_rows))
```

```python
import math

import jax
import jax.numpy as jnp
import numpy as np
from jax import lax
from jax.experimental import pallas as pl
from jax.experimental.pallas import tpu as pltpu
from jax.sharding import PartitionSpec as P

HEADS = 64
KVH = 8
HD = 128
PASSAGE = 512
BLOCK_PASSAGES = 2
SEQ_BLOCKS = 16
ROWS = 64
REQS = 4
CTX = 8
SPAN = BLOCK_PASSAGES * PASSAGE
BASE = 500000.0

MESH = pl.DeviceIdType.MESH
F32 = jnp.float32
BF16 = jnp.bfloat16
LOG2_SCALE = math.log2(math.e) / math.sqrt(HD)
NEG = -1e30
FAR = 1 << 30
STEPS = 4


def frequency_table():
    exponent = np.arange(HD // 2, dtype=np.float32) * np.float32(-2.0 * math.log(BASE) / HD)
    return np.exp(exponent.astype(np.float64)).astype(np.float32)


def passage_tables():
    offsets = np.arange(SEQ_BLOCKS * BLOCK_PASSAGES).astype(np.float32) * np.float32(PASSAGE)
    angles = (offsets[:, None] * frequency_table()[None, :]).astype(np.float64)
    cosine, sine = np.cos(angles), np.sin(angles)
    return (
        np.concatenate([cosine, cosine], axis=1).astype(np.float32),
        np.concatenate([-sine, sine], axis=1).astype(np.float32),
    )


def turned(vectors, cosine, signed_sine):
    half = HD // 2
    swapped = jnp.concatenate([vectors[:, half:], vectors[:, :half]], axis=1)
    return vectors * cosine + swapped * signed_sine


def iota(shape, axis):
    return lax.broadcasted_iota(jnp.int32, shape, axis)


def kernel(
    lists, slots, rec_ref, q_ref, fkv_ref, pool_ref, freq_ref, cos_ref, sin_ref,
    out_ref, dev_ref,
    pack, kvb, vt, kpos, fkv, fkv_in, vtf, fpos, recs, qown, qbuf, kf_own, kfbuf,
    part, pstat, osend, ssend, orecv, srecv, dsend, drecv, xbuf,
    kv_ss, kv_rs, rec_ss, rec_rs, f_ss, f_rs, q_ss, q_rs, kf_ss, kf_rs,
    o_ss, o_rs, s_ss, s_rs, d_ss, d_rs, x_ss, x_rs,
):
    where = lax.axis_index("pool")
    me_ctx = lax.axis_index("ctx")
    y = where // SEQ_BLOCKS
    z = where % SEQ_BLOCKS

    def node(row, column):
        return {"pool": (row % REQS) * SEQ_BLOCKS + (column + SEQ_BLOCKS) % SEQ_BLOCKS}

    def remote(src, dst, send, recv, target):
        return pltpu.make_async_remote_copy(
            src_ref=src, dst_ref=dst, send_sem=send, recv_sem=recv,
            device_id=target, device_id_type=MESH,
        )

    barrier = pltpu.get_barrier_semaphore()

    def greet(target):
        pl.semaphore_signal(barrier, inc=1, device_id=target, device_id_type=MESH)

    for k in range(1, SEQ_BLOCKS):
        greet(node(y, z + k))
    for row in range(1, REQS):
        for column in (-1, 0, 1):
            greet(node(y + row, z + column))
    for k in range(1, CTX):
        greet({"ctx": (me_ctx + k) % CTX})

    rec_row = rec_ref[...]
    rec_pair = jnp.concatenate([rec_row, rec_row], axis=1)
    recs[z] = rec_pair
    diagonal = iota((HD, HD), 0) == iota((HD, HD), 1)

    def as_column(row):
        wide = jnp.broadcast_to(row.astype(F32), (HD, HD))
        return jnp.sum(jnp.where(diagonal, wide, 0.0), axis=1, keepdims=True)

    rows_at = as_column(rec_pair)[:ROWS] + (z * SPAN).astype(F32)
    angles = rows_at * freq_ref[...]
    cosine = jnp.cos(angles)
    sine = jnp.where(iota((ROWS, HD), 1) < HD // 2, -jnp.sin(angles), jnp.sin(angles))
    for pair in range(4):
        both = [
            turned(q_ref[:, (2 * pair + i) * HD : (2 * pair + i + 1) * HD].astype(F32), cosine, sine)
            for i in range(2)
        ]
        stacked = jnp.concatenate(both, axis=0)
        qown[pair // 2, :, (pair % 2) * HD : (pair % 2 + 1) * HD] = stacked.T.astype(BF16)
    fresh_key = turned(fkv_ref[:, :HD].astype(F32), cosine, sine).astype(BF16)
    kf_own[...] = fresh_key
    fkv[:, :HD] = fresh_key
    fkv[:, HD:] = fkv_ref[:, HD:]

    @pl.loop(0, REQS)
    def _(request):
        @pl.loop(0, SEQ_BLOCKS)
        def _(block):
            keys, values = [], []
            for p in range(BLOCK_PASSAGES):
                passage = block * BLOCK_PASSAGES + p
                stored = pool_ref[slots[lists[request, passage]]]
                keys.append(
                    turned(
                        stored[:, :HD].astype(F32),
                        cos_ref[pl.ds(passage, 1), :],
                        sin_ref[pl.ds(passage, 1), :],
                    )
                )
                values.append(stored[:, HD:].astype(F32))
            pack[request, block, :, :HD] = jnp.concatenate(keys, axis=0).astype(BF16)
            pack[request, block, :, HD:] = jnp.concatenate(values, axis=0).astype(BF16)

    pl.semaphore_wait(barrier, SEQ_BLOCKS - 1 + 3 * (REQS - 1) + CTX - 1)

    def q_copy(d, s, c):
        src = qown.at[c] if s == 0 else qbuf.at[d, s - 1, c]
        return remote(
            src, qbuf.at[d, s, c], q_ss.at[d, s, c], q_rs.at[d, s, c], node(y, z + (2 - 4 * d))
        )

    def kf_copy(d, s):
        src = kf_own if s == 0 else kfbuf.at[d, s - 1]
        return remote(src, kfbuf.at[d, s], kf_ss.at[d, s], kf_rs.at[d, s], node(y, z + (2 - 4 * d)))

    def side(row_a, row_b):
        return 2 * (((row_a + row_b) % 4) // 2) - 1

    def kv_copy(i, step):
        row = (y + step) % REQS
        shift = side(y, row) if i else 0
        slot = i * REQS + y
        return remote(
            pack.at[row], kvb.at[:, slot], kv_ss.at[i, step], kv_rs.at[slot], node(row, z + shift)
        )

    def rec_copy(k):
        return remote(recs.at[z], recs.at[z], rec_ss.at[k], rec_rs.at[z], node(y, z + k))

    def fresh_copy():
        return remote(fkv, fkv_in, f_ss.at[0], f_rs.at[0], node(y, z + 1))

    def out_copies(d, s, c):
        target = node(y, z - (2 - 4 * d))
        return (
            remote(ssend.at[d, s, c], srecv.at[d, s, c], s_ss.at[d, s, c], s_rs.at[d, s, c], target),
            remote(osend.at[d, s, c], orecv.at[d, s, c], o_ss.at[d, s, c], o_rs.at[d, s, c], target),
        )

    def dev_copy(k):
        return remote(dsend.at[k], drecv.at[k], d_ss.at[k], d_rs.at[k], node(y, z - 2 * k))

    def ctx_copy(k):
        return remote(
            xbuf.at[me_ctx], xbuf.at[me_ctx], x_ss.at[k], x_rs.at[me_ctx],
            {"ctx": (me_ctx + k) % CTX},
        )

    own_kv = pltpu.make_async_copy(pack.at[y], kvb.at[:, y], kv_rs.at[y])

    for k in range(1, SEQ_BLOCKS):
        rec_copy(k).start()
    for c in range(2):
        for d in range(2):
            q_copy(d, 0, c).start()
    own_kv.start()
    for step in range(1, REQS):
        kv_copy(0, step).start()
    for step in range(REQS):
        kv_copy(1, step).start()
    for d in range(2):
        kf_copy(d, 0).start()
    fresh_copy().start()

    def rec_wait(k):
        other = (z + k) % SEQ_BLOCKS
        remote(recs.at[z], recs.at[other], rec_ss.at[k], rec_rs.at[other], node(y, z + k)).wait_recv()

    for k in range(1, SEQ_BLOCKS):
        rec_wait(k)
    key = iota((HD, HD), 0)
    key_row = (key >> 4) & 3
    key_side = ((y + key_row) & 3) & 2
    key_column = (z - (key >> 6) * (key_side - 1) + SEQ_BLOCKS) & (SEQ_BLOCKS - 1)
    offset = ((key >> 3) & 1) * PASSAGE + key_row * 128 + key_column * 8 + (key & 7)

    @pl.loop(0, SEQ_BLOCKS)
    def _(block):
        same = jnp.where(offset == recs[block], 1.0, 0.0)
        replaced = jnp.max(same, axis=1, keepdims=True) > 0.0
        kpos[block] = jnp.where(replaced, FAR, offset + block * SPAN)

    before = (z + SEQ_BLOCKS - 1) % SEQ_BLOCKS
    fresh_row = jnp.where(
        iota((1, HD), 1) < ROWS, recs[z] + z * SPAN, recs[before] + before * SPAN
    )
    fpos[...] = jnp.broadcast_to(as_column(fresh_row), (HD, HD)).astype(jnp.int32)

    def forward(s, everything):
        for c in range(2):
            for d in range(2):
                q_copy(d, s, c).wait_recv()
                if everything or c == d:
                    q_copy(d, s + 1, c).start()
        for d in range(2):
            kf_copy(d, s).wait_recv()
            if everything or d == 0:
                kf_copy(d, s + 1).start()

    def advance(carried, query, seen, keys, values_t):
        top, total, acc = carried
        scores = jnp.dot(keys, query, preferred_element_type=F32)
        scores = jnp.where(jnp.concatenate([seen, seen], axis=1), scores, NEG)
        new_top = jnp.maximum(top, jnp.max(scores, axis=0, keepdims=True))
        weights = jnp.exp2((scores - new_top) * LOG2_SCALE)
        factor = jnp.exp2((top - new_top) * LOG2_SCALE)
        total = total * factor + jnp.sum(weights, axis=0, keepdims=True)
        acc = acc * factor + jnp.dot(values_t, weights.astype(BF16), preferred_element_type=F32)
        return new_top, total, acc

    def attend(tile, query, slot):
        at = recs[tile] + tile * SPAN
        fresh_keys = jnp.concatenate([fkv[:, :HD], fkv_in[:, :HD]], axis=0)
        start = (
            jnp.full((1, 2 * HD), NEG, F32),
            jnp.zeros((1, 2 * HD), F32),
            jnp.zeros((HD, 2 * HD), F32),
        )
        carried = advance(start, query, fpos[...] <= at, fresh_keys, vtf[...])

        def group(g, carried):
            keys = kvb[pl.ds(2 * g, 2), :, :, :HD].reshape(2 * HD, HD)
            seen = kpos[pl.ds(2 * g, 2)].reshape(2 * HD, HD) <= at
            return advance(carried, query, seen, keys, vt[g])

        top, total, acc = lax.fori_loop(0, tile // 2 + 1, group, carried)
        part[slot] = acc
        pstat[slot, 0:1, :] = top
        pstat[slot, 1:2, :] = total

    def gap_of(tile, keys, k):
        same = jnp.where(offset == recs[tile], 1.0, 0.0)[:, :ROWS].astype(BF16)
        cached = kvb[pl.ds(tile, 1), :, :, :HD].reshape(HD, HD)
        over = (((0,), (0,)), ((), ()))
        found = lax.dot_general(same, cached, over, preferred_element_type=F32)
        hit = lax.dot_general(same, jnp.ones((HD, HD), BF16), over, preferred_element_type=F32)
        gap = (found - keys.astype(F32)) * hit
        squares = (gap * gap).T
        dsend[k, :, :ROWS] = jnp.sum(squares, axis=0, keepdims=True)

    def tile_of(d, s):
        return (z - (2 - 4 * d) * (s + 1) + SEQ_BLOCKS) % SEQ_BLOCKS

    def jobs(s, first, count):
        @pl.loop(first, first + count)
        def _(i):
            d, c = i % 2, i // 2
            attend(tile_of(d, s), qbuf[d, s, c], (s * 2 + d) * 2 + c)

    def far_jobs():
        @pl.loop(0, 2)
        def _(d):
            s = STEPS - 1
            attend(tile_of(d, s), qbuf[d, s, d], (s * 2 + d) * 2 + d)

    def gaps(s):
        for d in range(2):
            if s == STEPS - 1 and d:
                continue
            k = s + 1 if d == 0 else SEQ_BLOCKS // 2 - s - 1
            gap_of(tile_of(d, s), kfbuf[d, s], k)
            dev_copy(k).start()

    dsend[...] = jnp.zeros_like(dsend)
    forward(0, True)

    for slot in range(2 * REQS):
        pltpu.make_async_copy(pack.at[0], kvb.at[:, slot], kv_rs.at[slot]).wait()
    fresh_copy().wait_recv()

    @pl.loop(0, SEQ_BLOCKS // 2)
    def _(g):
        for i in range(2):
            values = kvb[pl.ds(2 * g + i, 1), :, :, HD:].reshape(HD, HD)
            vt[g, :, i * HD : (i + 1) * HD] = values.astype(F32).T.astype(BF16)

    fresh_values = jnp.concatenate([fkv[:, HD:], fkv_in[:, HD:]], axis=0)
    vtf[...] = fresh_values.astype(F32).T.astype(BF16)

    @pl.loop(0, 2)
    def _(c):
        attend(z, qown[c], 16 + c)

    forward(1, True)
    jobs(0, 0, 4)
    gap_of(z, kf_own[...], 0)
    gaps(0)
    forward(2, False)
    jobs(1, 0, 4)
    gaps(1)
    jobs(2, 0, 4)

    def merged(d, s, c, slot):
        top, total, acc = pstat[slot, 0:1, :], pstat[slot, 1:2, :], part[slot]
        stats, far = out_copies(d, s, c)
        stats.wait_recv()
        other = srecv[d, s, c]
        other_top = jnp.concatenate([other[0:1, :], other[1:2, :]], axis=1)
        other_total = jnp.concatenate([other[2:3, :], other[3:4, :]], axis=1)
        new_top = jnp.maximum(top, other_top)
        mine = jnp.exp2((top - new_top) * LOG2_SCALE)
        theirs = jnp.exp2((other_top - new_top) * LOG2_SCALE)
        total = total * mine + other_total * theirs
        far.wait_recv()
        acc = acc * mine + orecv[d, s, c].astype(F32) * theirs
        return new_top, total, acc

    def hand_on(d, s, c):
        slot = (s * 2 + d) * 2 + c
        if s == STEPS - 1 or (s == STEPS - 2 and c != d):
            top, total, acc = pstat[slot, 0:1, :], pstat[slot, 1:2, :], part[slot]
        else:
            top, total, acc = merged(d, s + 1, c, slot)
        ssend[d, s, c, 0:1, :] = top[:, :HD]
        ssend[d, s, c, 1:2, :] = top[:, HD:]
        ssend[d, s, c, 2:3, :] = total[:, :HD]
        ssend[d, s, c, 3:4, :] = total[:, HD:]
        osend[d, s, c] = acc.astype(BF16)
        for copy in out_copies(d, s, c):
            copy.start()

    ssend[...] = jnp.zeros_like(ssend)
    for d in range(2):
        hand_on(d, 2, 1 - d)
    for d in range(2):
        q_copy(d, 3, d).wait_recv()
    far_jobs()
    for d in range(2):
        hand_on(d, 3, d)
    kf_copy(0, 3).wait_recv()
    gaps(2)
    gaps(3)
    for d in range(2):
        hand_on(d, 1, 1 - d)
    for k in range(1, 8):
        dev_copy(k).wait_recv()
    shared = dsend[0]
    for k in range(1, 8):
        shared = shared + drecv[k]
    xbuf[me_ctx] = shared
    for k in range(1, CTX):
        ctx_copy(k).start()
    for d in range(2):
        hand_on(d, 2, d)
    for d in range(2):
        hand_on(d, 0, 1 - d)
    for d in range(2):
        hand_on(d, 1, d)
    for d in range(2):
        hand_on(d, 0, d)

    for k in range(1, CTX):
        other = (me_ctx + k) % CTX
        remote(
            xbuf.at[me_ctx], xbuf.at[other], x_ss.at[k], x_rs.at[other], {"ctx": other}
        ).wait_recv()
    gathered = xbuf[0]
    for k in range(1, CTX):
        gathered = gathered + xbuf[k]
    dev_ref[...] = gathered[:, :ROWS] / (KVH * HD)

    for c in range(2):
        slot = 16 + c
        for d in ((0, 1) if c else (1, 0)):
            top, total, acc = merged(d, 0, c, slot)
            pstat[slot, 0:1, :] = top
            pstat[slot, 1:2, :] = total
            part[slot] = acc
        done = part[slot] / pstat[slot, 1:2, :]
        for pair in range(2):
            upright = done[:, pair * HD : (pair + 1) * HD].T.astype(BF16)
            for i in range(2):
                head = c * 4 + pair * 2 + i
                out_ref[:, head * HD : (head + 1) * HD] = upright[i * ROWS : (i + 1) * ROWS]

    for k in range(1, SEQ_BLOCKS):
        rec_copy(k).wait_send()
    for step in range(REQS):
        if step:
            kv_copy(0, step).wait_send()
        kv_copy(1, step).wait_send()
    fresh_copy().wait_send()
    for d in range(2):
        for s in range(STEPS):
            for c in range(2):
                if s < STEPS - 1 or c == d:
                    q_copy(d, s, c).wait_send()
                    for copy in out_copies(d, s, c):
                        copy.wait_send()
            if s < STEPS - 1 or d == 0:
                kf_copy(d, s).wait_send()
    for k in range(1, 8):
        dev_copy(k).wait_send()
    for k in range(1, CTX):
        ctx_copy(k).wait_send()


def on_device(fresh_q, fresh_kv, pool_kv, passage_lists, slot_map, rec_pos):
    freq = frequency_table()
    freq = jnp.asarray(np.concatenate([freq, freq])[None, :])
    cosine, sine = (jnp.asarray(table) for table in passage_tables())
    vmem = pl.BlockSpec(memory_space=pltpu.VMEM)
    smem = pl.BlockSpec(memory_space=pltpu.SMEM)
    dma = pltpu.SemaphoreType.DMA
    output, deviation = pl.pallas_call(
        kernel,
        out_shape=(
            jax.ShapeDtypeStruct((ROWS, HEADS // CTX * HD), BF16),
            jax.ShapeDtypeStruct((1, ROWS), F32),
        ),
        in_specs=[smem, smem] + [vmem] * 7,
        out_specs=(vmem, vmem),
        scratch_shapes=[
            pltpu.VMEM((REQS, SEQ_BLOCKS, 16, 2 * HD), BF16),
            pltpu.VMEM((SEQ_BLOCKS, 2 * REQS, 16, 2 * HD), BF16),
            pltpu.VMEM((SEQ_BLOCKS // 2, HD, 2 * HD), BF16),
            pltpu.VMEM((SEQ_BLOCKS, HD, HD), jnp.int32),
            pltpu.VMEM((ROWS, 2 * HD), BF16),
            pltpu.VMEM((ROWS, 2 * HD), BF16),
            pltpu.VMEM((HD, HD), BF16),
            pltpu.VMEM((HD, HD), jnp.int32),
            pltpu.VMEM((SEQ_BLOCKS, 1, HD), jnp.int32),
            pltpu.VMEM((2, HD, 2 * HD), BF16),
            pltpu.VMEM((2, STEPS, 2, HD, 2 * HD), BF16),
            pltpu.VMEM((ROWS, HD), BF16),
            pltpu.VMEM((2, STEPS, ROWS, HD), BF16),
            pltpu.VMEM((18, HD, 2 * HD), F32),
            pltpu.VMEM((18, 8, 2 * HD), F32),
            pltpu.VMEM((2, STEPS, 2, HD, 2 * HD), BF16),
            pltpu.VMEM((2, STEPS, 2, 8, HD), F32),
            pltpu.VMEM((2, STEPS, 2, HD, 2 * HD), BF16),
            pltpu.VMEM((2, STEPS, 2, 8, HD), F32),
            pltpu.VMEM((8, 1, HD), F32),
            pltpu.VMEM((8, 1, HD), F32),
            pltpu.VMEM((CTX, 1, HD), F32),
            dma((2, REQS)), dma((2 * REQS,)),
            dma((SEQ_BLOCKS,)), dma((SEQ_BLOCKS,)),
            dma((1,)), dma((1,)),
            dma((2, STEPS, 2)), dma((2, STEPS, 2)),
            dma((2, STEPS)), dma((2, STEPS)),
            dma((2, STEPS, 2)), dma((2, STEPS, 2)),
            dma((2, STEPS, 2)), dma((2, STEPS, 2)),
            dma((8,)), dma((8,)),
            dma((CTX,)), dma((CTX,)),
        ],
        compiler_params=pltpu.CompilerParams(
            collective_id=0, has_side_effects=True, vmem_limit_bytes=40 * 2**20
        ),
    )(passage_lists, slot_map, rec_pos, fresh_q, fresh_kv, pool_kv, freq, cosine, sine)
    return output, deviation.reshape(ROWS)


def solution(mesh):
    in_specs = (
        P("pool", "ctx"),
        P("pool", "ctx"),
        P(None, "pool", "ctx"),
        P(),
        P(),
        P("pool", None),
    )
    out_specs = (P("pool", "ctx"), P("pool"))
    return jax.shard_map(
        on_device, mesh=mesh, in_specs=in_specs, out_specs=out_specs, check_vma=False
    )
```

```python
import math

import jax
import jax.numpy as jnp
import numpy as np
from jax import lax
from jax.experimental import pallas as pl
from jax.experimental.pallas import tpu as pltpu
from jax.sharding import PartitionSpec as P

HEADS = 64
KVH = 8
HD = 128
PASSAGE = 512
BLOCK_PASSAGES = 2
SEQ_BLOCKS = 16
ROWS = 64
REQS = 4
CTX = 8
SPAN = BLOCK_PASSAGES * PASSAGE
BASE = 500000.0

MESH = pl.DeviceIdType.MESH
F32 = jnp.float32
BF16 = jnp.bfloat16
LOG2_SCALE = math.log2(math.e) / math.sqrt(HD)
NEG = -1e30
FAR = 1 << 30
WIDE = 4 * HD
PIECE = 4
GROUP = 4
STEPS = 4


def frequency_table():
    exponent = np.arange(HD // 2, dtype=np.float32) * np.float32(-2.0 * math.log(BASE) / HD)
    return np.exp(exponent.astype(np.float64)).astype(np.float32)


def angle_table():
    freq = frequency_table()
    offsets = np.arange(SEQ_BLOCKS * BLOCK_PASSAGES).astype(np.float32) * np.float32(PASSAGE)
    angles = (offsets[:, None] * freq[None, :]).astype(np.float64)
    cosine, sine = np.cos(angles), np.sin(angles)
    rows = [
        np.concatenate([cosine, cosine], axis=1),
        np.concatenate([-sine, sine], axis=1),
        np.tile(freq, 2)[None, :],
        np.zeros((7, HD)),
    ]
    return np.concatenate(rows, axis=0).astype(np.float32)


def turned(vectors, cosine, signed_sine):
    half = HD // 2
    swapped = jnp.concatenate([vectors[:, half:], vectors[:, :half]], axis=1)
    return vectors * cosine + swapped * signed_sine


def iota(shape, axis):
    return lax.broadcasted_iota(jnp.int32, shape, axis)


def kernel(
    lists_in, slots_in, rec_in, q_in, fkv_in, pool_in, table_in,
    out_ref, dev_ref,
    lists, slots, rec_ref, q_ref, fkv_ref, pool_ref, table,
    pack, kvb, vt, kpos, fkv, fkv_next, vtf, fpos, recs, qown, qbuf,
    kf_own, meta, sbuf, wbuf, part, pstat, osend, ssend, orecv, srecv, dsend, drecv, cbuf, xbuf,
    ready, ready_4, ready_8, in_s, kv_ss, kv_rs, rec_ss, rec_rs, f_ss, f_rs, q_ss, q_rs, m_ss, m_rs,
    o_ss, o_rs, s_ss, s_rs, d_ss, d_rs, c_ss, c_rs, x_ss, x_rs,
):
    where = lax.axis_index("pool")
    me_ctx = lax.axis_index("ctx")
    y = where >> 4
    z = where & (SEQ_BLOCKS - 1)

    def node(row, column):
        return {"pool": ((row & (REQS - 1)) << 4) + ((column + SEQ_BLOCKS) & (SEQ_BLOCKS - 1))}

    def remote(src, dst, send, recv, target):
        return pltpu.make_async_remote_copy(
            src_ref=src, dst_ref=dst, send_sem=send, recv_sem=recv,
            device_id=target, device_id_type=MESH,
        )

    inputs = [
        pltpu.make_async_copy(src, dst, in_s.at[i])
        for i, (src, dst) in enumerate(
            [
                (q_in, q_ref), (rec_in, rec_ref), (table_in, table), (fkv_in, fkv_ref),
                (lists_in, lists), (slots_in, slots), (pool_in, pool_ref),
            ]
        )
    ]
    for copy in inputs:
        copy.start()

    barrier = pltpu.get_barrier_semaphore()

    def greet(target):
        pl.semaphore_signal(barrier, inc=1, device_id=target, device_id_type=MESH)

    chips = CTX // 2
    core, chip = me_ctx & 1, me_ctx >> 1

    def same_core(k):
        return ((chip + k) & (chips - 1)) * 2 + core

    for k in (-2, -1, 1, 2):
        greet(node(y, z + k))
    for row in range(1, REQS):
        greet(node(y + row, z))
    greet({"ctx": me_ctx + 1 - 2 * core})
    for k in range(1, chips):
        greet({"ctx": same_core(k)})

    for copy in inputs[:4]:
        copy.wait()
    rec_row = rec_ref[...]
    rec_pair = jnp.concatenate([rec_row, rec_row], axis=1)
    recs[z] = rec_pair
    diagonal = iota((HD, HD), 0) == iota((HD, HD), 1)

    def as_column(row):
        wide = jnp.broadcast_to(row.astype(F32), (HD, HD))
        return jnp.sum(jnp.where(diagonal, wide, 0.0), axis=1, keepdims=True)

    rows_at = as_column(rec_pair)[:ROWS] + (z * SPAN).astype(F32)
    angles = rows_at * table[64:65, :]
    cosine = jnp.cos(angles)
    sine = jnp.sin(angles)
    sine = jnp.where(iota((ROWS, HD), 1) < HD // 2, -sine, sine)
    for pair in range(4):
        both = [
            turned(q_ref[:, (2 * pair + i) * HD : (2 * pair + i + 1) * HD].astype(F32), cosine, sine)
            for i in range(2)
        ]
        stacked = jnp.concatenate(both, axis=0)
        qown[pair] = stacked.T.astype(BF16)
    fresh_key = turned(fkv_ref[:, :HD].astype(F32), cosine, sine).astype(BF16)
    kf_own[...] = fresh_key
    fkv[:, :HD] = fresh_key
    fkv[:, HD:] = fkv_ref[:, HD:]
    for copy in inputs[4:]:
        copy.wait()

    def pack_for(request):
        @pl.loop(0, SEQ_BLOCKS, unroll=16)
        def _(block):
            keys, values = [], []
            for p in range(BLOCK_PASSAGES):
                passage = block * BLOCK_PASSAGES + p
                stored = pool_ref[slots[lists[request, passage]]]
                keys.append(
                    turned(
                        stored[:, :HD].astype(F32),
                        table[pl.ds(passage, 1), :],
                        table[pl.ds(passage + 32, 1), :],
                    )
                )
                values.append(stored[:, HD:].astype(F32))
            pack[request, block, :, :HD] = jnp.concatenate(keys, axis=0).astype(BF16)
            pack[request, block, :, HD:] = jnp.concatenate(values, axis=0).astype(BF16)

    for step in range(REQS):
        pack_for(step)

    pl.semaphore_wait(barrier, 4 + (REQS - 1) + 1 + chips - 1)
    for row in range(1, REQS):
        pl.semaphore_signal(ready, inc=1, device_id=node(y + row, z), device_id_type=MESH)
    for k in (-2, 2):
        pl.semaphore_signal(ready_4, inc=1, device_id=node(y, z + k), device_id_type=MESH)

    def along(d):
        return node(y, z + (2 - 4 * d))

    def q_copy(d, s, c):
        src = qown.at[c] if s == 0 else qbuf.at[d, s - 1, c]
        return remote(src, qbuf.at[d, s, c], q_ss.at[d, s, c], q_rs.at[d, s, c], along(d))

    def in_turn(first=0, count=4):
        return [((k + 2 * d) % 4, d) for k in range(first, first + count) for d in range(2)]

    def meta_copy(d, s):
        src = kf_own if s == 0 else meta.at[d, s - 1]
        return remote(src, meta.at[d, s], m_ss.at[d, s], m_rs.at[d, s], along(d))

    def side(row_a, row_b):
        return ((row_a + row_b) & 2) - 1

    def kv_copy(i, step, first=0, count=SEQ_BLOCKS):
        row = (y + step) & (REQS - 1)
        shift = side(y, row) if i else 0
        slot = i * REQS + y
        blocks = pl.ds(first, count)
        return remote(
            pack.at[row, blocks], kvb.at[blocks, slot], kv_ss.at[i, step], kv_rs.at[slot],
            node(row, z + shift),
        )

    def rec_copy(k):
        return remote(recs.at[z], recs.at[z], rec_ss.at[k], rec_rs.at[z], node(y, z + k))

    def fresh_copy():
        return remote(fkv, fkv_next, f_ss.at[0], f_rs.at[0], node(y, z + 1))

    def stat_copy(d, s, h):
        return remote(
            ssend.at[d, s, h], srecv.at[d, s, h], s_ss.at[d, s, h], s_rs.at[d, s, h], along(1 - d)
        )

    def out_copy(d, s, c):
        return remote(
            osend.at[d, s, c], orecv.at[d, s, c], o_ss.at[d, s, c], o_rs.at[d, s, c], along(1 - d)
        )

    def dev_copy(k):
        return remote(dsend.at[k], drecv.at[k], d_ss.at[k], d_rs.at[k], node(y, z - 2 * k))

    def core_copy():
        return remote(cbuf.at[0], cbuf.at[1], c_ss.at[0], c_rs.at[0], {"ctx": me_ctx + 1 - 2 * core})

    def chip_copy(k):
        return remote(
            xbuf.at[chip], xbuf.at[chip], x_ss.at[k], x_rs.at[chip], {"ctx": same_core(k)}
        )

    own_kv = pltpu.make_async_copy(pack.at[y], kvb.at[:, y], kv_rs.at[y])
    for c, d in in_turn(0, 2):
        q_copy(d, 0, c).start()
    own_kv.start()

    def kv_piece(i, n):
        for step in (2, 1, 3, 0):
            if i or step:
                kv_copy(i, step, n * PIECE, PIECE).start()

    kv_piece(0, 0)
    for c, d in in_turn(2, 1):
        q_copy(d, 0, c).start()
    pl.semaphore_wait(ready, REQS - 1)
    kv_piece(1, 0)
    for c, d in in_turn(3, 1):
        q_copy(d, 0, c).start()
    pl.semaphore_wait(ready_4, 2)
    for k in (-4, 4):
        pl.semaphore_signal(ready_8, inc=1, device_id=node(y, z + k), device_id_type=MESH)
    for i in range(2):
        kv_piece(i, 1)
    pl.semaphore_wait(ready_8, 2)
    for k in (8, 7, 9, 6, 10, 5, 11, 4, 12, 3, 13, 2, 14, 1, 15):
        rec_copy(k).start()
    for n in (2, 3):
        for i in range(2):
            kv_piece(i, n)
    for d in range(2):
        meta_copy(d, 0).start()
    fresh_copy().start()

    def q_on(d, s, c):
        q_copy(d, s, c).wait_recv()
        if s < STEPS - 2 or (s == STEPS - 2 and c // 2 == d):
            q_copy(d, s + 1, c).start()

    def meta_on(d, s):
        meta_copy(d, s).wait_recv()
        if s < STEPS - 2 or (s == STEPS - 2 and d == 0):
            meta_copy(d, s + 1).start()

    key = iota((HD, HD), 0)
    key_row = (key >> 4) & 3
    key_side = ((y + key_row) & 3) & 2
    key_column = (z - (key >> 6) * (key_side - 1) + SEQ_BLOCKS) & (SEQ_BLOCKS - 1)
    offset = ((key >> 3) & 1) * PASSAGE + key_row * 128 + key_column * 8 + (key & 7)

    def tile_of(d, s):
        return (z - (2 - 4 * d) * (s + 1) + SEQ_BLOCKS) & (SEQ_BLOCKS - 1)

    def step_on(s):
        for c, d in in_turn():
            q_on(d, s, c)
        for d in range(2):
            meta_on(d, s)

    step_on(0)
    for k in range(1, SEQ_BLOCKS):
        other = (z + k) & (SEQ_BLOCKS - 1)
        remote(
            recs.at[z], recs.at[other], rec_ss.at[k], rec_rs.at[other], node(y, z + k)
        ).wait_recv()

    @pl.loop(0, SEQ_BLOCKS, unroll=2)
    def _(block):
        same = jnp.where(offset == recs[block], 1.0, 0.0)
        replaced = jnp.max(same, axis=1, keepdims=True) > 0.0
        kpos[block] = jnp.where(replaced, FAR, offset + block * SPAN)

    before = (z + SEQ_BLOCKS - 1) & (SEQ_BLOCKS - 1)
    fresh_row = jnp.where(
        iota((1, HD), 1) < ROWS, recs[z] + z * SPAN, recs[before] + before * SPAN
    )
    fpos[...] = jnp.broadcast_to(as_column(fresh_row), (HD, HD)).astype(jnp.int32)

    step_on(1)

    for slot in range(2 * REQS):
        pltpu.make_async_copy(pack.at[0], kvb.at[:, slot], kv_rs.at[slot]).wait()
    fresh_copy().wait_recv()

    @pl.loop(0, SEQ_BLOCKS // GROUP)
    def _(g):
        for i in range(GROUP):
            values = kvb[pl.ds(GROUP * g + i, 1), :, :, HD:].reshape(HD, HD)
            vt[g, :, i * HD : (i + 1) * HD] = values.astype(F32).T.astype(BF16)

    fresh_values = jnp.concatenate([fkv[:, HD:], fkv_next[:, HD:]], axis=0)
    vtf[...] = fresh_values.astype(F32).T.astype(BF16)

    def score(query, at, blocks):
        top = None
        for i, (keys, places) in enumerate(blocks):
            seen = places <= at
            scores = jnp.dot(keys, query, preferred_element_type=F32)
            scores = jnp.where(jnp.concatenate([seen] * 4, axis=1), scores, NEG)
            sbuf[i] = scores
            largest = jnp.max(scores.reshape(HD // 8, 8, WIDE), axis=0)
            top = largest if top is None else jnp.maximum(top, largest)
        return jnp.max(top, axis=0, keepdims=True)

    def weigh(top, count):
        total = None
        for i in range(count):
            weights = jnp.exp2((sbuf[i] - top) * LOG2_SCALE)
            summed = jnp.sum(weights.reshape(HD // 8, 8, WIDE), axis=0)
            total = summed if total is None else total + summed
            wbuf[i * HD : (i + 1) * HD, :] = weights.astype(BF16)
        return jnp.sum(total, axis=0, keepdims=True)

    def stored(g):
        return [
            (kvb[g * GROUP + i, :, :, :HD].reshape(HD, HD), kpos[g * GROUP + i])
            for i in range(GROUP)
        ]

    def attend(tile, queries, job):
        at = recs[tile] + tile * SPAN
        query = jnp.concatenate([one[...] for one in queries], axis=1)
        fresh_keys = jnp.concatenate([fkv[:, :HD], fkv_next[:, :HD]], axis=0)
        top = score(query, at, [(fresh_keys, fpos[...])] + stored(0))
        total = weigh(top, GROUP + 1)
        part[job] = jnp.dot(vtf[...], wbuf[:HD, :], preferred_element_type=F32) + jnp.dot(
            vt[0], wbuf[HD:, :], preferred_element_type=F32
        )
        pstat[job, 0:1, :] = top
        pstat[job, 1:2, :] = total

        @pl.loop(1, (tile >> 2) + 1)
        def _(g):
            old_top = pstat[job, 0:1, :]
            top = jnp.maximum(old_top, score(query, at, stored(g)))
            total = weigh(top, GROUP)
            factor = jnp.exp2((old_top - top) * LOG2_SCALE)
            part[job] = part[job] * factor + jnp.dot(
                vt[g], wbuf[: GROUP * HD, :], preferred_element_type=F32
            )
            pstat[job, 0:1, :] = top
            pstat[job, 1:2, :] = pstat[job, 1:2, :] * factor + total

    def job_of(d, s):
        return 7 if s == STEPS - 1 else 1 + 2 * s + d

    def jobs(s):
        @pl.loop(0, 2)
        def _(d):
            attend(tile_of(d, s), [qbuf.at[d, s, c] for c in range(4)], 1 + 2 * s + d)

    def gap_of(tile, keys, k):
        same = jnp.where(offset == recs[tile], 1.0, 0.0)[:, :ROWS].astype(BF16)
        cached = kvb[pl.ds(tile, 1), :, :, :HD].reshape(HD, HD)
        over = (((0,), (0,)), ((), ()))
        found = lax.dot_general(same, cached, over, preferred_element_type=F32)
        hit = lax.dot_general(same, jnp.ones((HD, HD), BF16), over, preferred_element_type=F32)
        gap = (found - keys.astype(F32)) * hit
        squares = (gap * gap).T
        dsend[k, :, :ROWS] = jnp.sum(squares, axis=0, keepdims=True)

    def stats_of(job, h):
        columns = slice(h * 2 * HD, (h + 1) * 2 * HD)
        return pstat[job, 0:1, columns], pstat[job, 1:2, columns]

    def part_of(job, c):
        return part[job, :, c * HD : (c + 1) * HD]

    def combine(d, s, h, job):
        top, total = stats_of(job, h)
        stat_copy(d, s, h).wait_recv()
        other = srecv[d, s, h]
        other_top = jnp.concatenate([other[0:1, :], other[1:2, :]], axis=1)
        other_total = jnp.concatenate([other[2:3, :], other[3:4, :]], axis=1)
        new_top = jnp.maximum(top, other_top)
        mine = jnp.exp2((top - new_top) * LOG2_SCALE)
        theirs = jnp.exp2((other_top - new_top) * LOG2_SCALE)
        return new_top, total * mine + other_total * theirs, mine, theirs

    def summed(d, s, h, i, job, mine, theirs):
        columns = slice(i * HD, (i + 1) * HD)
        out_copy(d, s, 2 * h + i).wait_recv()
        far = orecv[d, s, 2 * h + i].astype(F32)
        return part_of(job, 2 * h + i) * mine[:, columns] + far * theirs[:, columns]

    def hand_on(s, furthest):
        first = s == STEPS - 1 or (s == STEPS - 2 and not furthest)
        factors = []
        for d in range(2):
            h = d if furthest else 1 - d
            job = job_of(d, s)
            if first:
                top, total = stats_of(job, h)
                factors.append(None)
            else:
                top, total, mine, theirs = combine(d, s + 1, h, job)
                factors.append((mine, theirs))
            ssend[d, s, h, 0:1, :] = top[:, :HD]
            ssend[d, s, h, 1:2, :] = top[:, HD:]
            ssend[d, s, h, 2:3, :] = total[:, :HD]
            ssend[d, s, h, 3:4, :] = total[:, HD:]
            stat_copy(d, s, h).start()
        for i in range(2):
            for d in range(2):
                h = d if furthest else 1 - d
                job = job_of(d, s)
                if first:
                    acc = part_of(job, 2 * h + i)
                else:
                    acc = summed(d, s + 1, h, i, job, *factors[d])
                osend[d, s, 2 * h + i] = acc.astype(BF16)
                out_copy(d, s, 2 * h + i).start()

    def gaps(s):
        for d in range(2 if s < STEPS - 1 else 1):
            k = s + 1 if d == 0 else SEQ_BLOCKS // 2 - s - 1
            gap_of(tile_of(d, s), meta[d, s], k)
            dev_copy(k).start()

    dsend[...] = jnp.zeros_like(dsend)
    attend(z, [qown.at[c] for c in range(4)], 0)
    jobs(0)
    step_on(2)
    jobs(1)
    jobs(2)
    for c, d in in_turn(0, 2):
        q_copy(d, 3, c).wait_recv()
    attend(tile_of(0, 3), [qbuf.at[c // 2, 3, c] for c in range(4)], 7)
    hand_on(3, True)
    hand_on(2, False)
    meta_copy(0, 3).wait_recv()
    gaps(3)
    gaps(2)
    hand_on(2, True)
    gaps(1)
    hand_on(1, False)
    gaps(0)
    gap_of(z, fkv[:, :HD], 0)
    hand_on(1, True)
    hand_on(0, False)
    for k in range(1, 8):
        dev_copy(k).wait_recv()
    shared = dsend[0]
    for k in range(1, 8):
        shared = shared + drecv[k]
    cbuf[0] = shared
    core_copy().start()
    hand_on(0, True)
    core_copy().wait_recv()
    xbuf[chip] = cbuf[0] + cbuf[1]
    for k in range(1, chips):
        chip_copy(k).start()

    def home(d, h):
        top, total, mine, theirs = combine(d, 0, h, 0)
        columns = slice(h * 2 * HD, (h + 1) * 2 * HD)
        pstat[0, 0:1, columns] = top
        pstat[0, 1:2, columns] = total
        for i in range(2):
            acc = summed(d, 0, h, i, 0, mine, theirs)
            part[0, :, (2 * h + i) * HD : (2 * h + i + 1) * HD] = acc

    for h in range(2):
        home(1 - h, h)
    for k in range(1, chips):
        other = (chip + k) & (chips - 1)
        remote(
            xbuf.at[chip], xbuf.at[other], x_ss.at[k], x_rs.at[other], {"ctx": same_core(k)}
        ).wait_recv()
    gathered = xbuf[0]
    for k in range(1, chips):
        gathered = gathered + xbuf[k]
    dev_ref[...] = gathered[:, :ROWS] / (KVH * HD)

    for h in range(2):
        home(h, h)
        for pair in range(2):
            columns = slice((2 * h + pair) * HD, (2 * h + pair + 1) * HD)
            upright = (part[0, :, columns] / pstat[0, 1:2, columns]).T.astype(BF16)
            for i in range(2):
                head = h * 4 + pair * 2 + i
                out_ref[:, head * HD : (head + 1) * HD] = upright[i * ROWS : (i + 1) * ROWS]

    for k in range(1, SEQ_BLOCKS):
        rec_copy(k).wait_send()
    for k in range(1, 8):
        dev_copy(k).wait_send()
    for step in range(REQS):
        if step:
            kv_copy(0, step).wait_send()
        kv_copy(1, step).wait_send()
    fresh_copy().wait_send()
    for d in range(2):
        for s in range(STEPS):
            for c in range(4):
                if s < STEPS - 1 or c // 2 == d:
                    q_copy(d, s, c).wait_send()
                    out_copy(d, s, c).wait_send()
                    if c % 2 == 0:
                        stat_copy(d, s, c // 2).wait_send()
            if s < STEPS - 1 or d == 0:
                meta_copy(d, s).wait_send()
    core_copy().wait_send()
    for k in range(1, chips):
        chip_copy(k).wait_send()


def on_device(fresh_q, fresh_kv, pool_kv, passage_lists, slot_map, rec_pos):
    vmem = pl.BlockSpec(memory_space=pltpu.VMEM)
    anywhere = pl.BlockSpec(memory_space=pl.ANY)
    dma = pltpu.SemaphoreType.DMA
    scratch = [
        pltpu.SMEM(passage_lists.shape, jnp.int32),
        pltpu.SMEM(slot_map.shape, jnp.int32),
        pltpu.VMEM(rec_pos.shape, jnp.int32),
        pltpu.VMEM(fresh_q.shape, BF16),
        pltpu.VMEM(fresh_kv.shape, BF16),
        pltpu.VMEM(pool_kv.shape, BF16),
        pltpu.VMEM((72, HD), F32),
        pltpu.VMEM((REQS, SEQ_BLOCKS, 16, 2 * HD), BF16),
        pltpu.VMEM((SEQ_BLOCKS, 2 * REQS, 16, 2 * HD), BF16),
        pltpu.VMEM((SEQ_BLOCKS // GROUP, HD, GROUP * HD), BF16),
        pltpu.VMEM((SEQ_BLOCKS, HD, HD), jnp.int32),
        pltpu.VMEM((ROWS, 2 * HD), BF16),
        pltpu.VMEM((ROWS, 2 * HD), BF16),
        pltpu.VMEM((HD, HD), BF16),
        pltpu.VMEM((HD, HD), jnp.int32),
        pltpu.VMEM((SEQ_BLOCKS, 1, HD), jnp.int32),
        pltpu.VMEM((4, HD, HD), BF16),
        pltpu.VMEM((2, STEPS, 4, HD, HD), BF16),
        pltpu.VMEM((ROWS, HD), BF16),
        pltpu.VMEM((2, STEPS, ROWS, HD), BF16),
        pltpu.VMEM((GROUP + 1, HD, WIDE), F32),
        pltpu.VMEM(((GROUP + 1) * HD, WIDE), BF16),
        pltpu.VMEM((8, HD, WIDE), F32),
        pltpu.VMEM((8, 8, WIDE), F32),
        pltpu.VMEM((2, STEPS, 4, HD, HD), BF16),
        pltpu.VMEM((2, STEPS, 2, 4, HD), F32),
        pltpu.VMEM((2, STEPS, 4, HD, HD), BF16),
        pltpu.VMEM((2, STEPS, 2, 4, HD), F32),
        pltpu.VMEM((8, 1, HD), F32),
        pltpu.VMEM((8, 1, HD), F32),
        pltpu.VMEM((2, 1, HD), F32),
        pltpu.VMEM((CTX // 2, 1, HD), F32),
        pltpu.SemaphoreType.REGULAR,
        pltpu.SemaphoreType.REGULAR,
        pltpu.SemaphoreType.REGULAR,
        dma((7,)),
        dma((2, REQS)), dma((2 * REQS,)),
        dma((SEQ_BLOCKS,)), dma((SEQ_BLOCKS,)),
        dma((1,)), dma((1,)),
        dma((2, STEPS, 4)), dma((2, STEPS, 4)),
        dma((2, STEPS)), dma((2, STEPS)),
        dma((2, STEPS, 4)), dma((2, STEPS, 4)),
        dma((2, STEPS, 2)), dma((2, STEPS, 2)),
        dma((8,)), dma((8,)),
        dma((1,)), dma((1,)),
        dma((CTX // 2,)), dma((CTX // 2,)),
    ]
    output, deviation = pl.pallas_call(
        kernel,
        out_shape=(
            jax.ShapeDtypeStruct((ROWS, HEADS // CTX * HD), BF16),
            jax.ShapeDtypeStruct((1, ROWS), F32),
        ),
        in_specs=[anywhere] * 7,
        out_specs=(vmem, vmem),
        scratch_shapes=scratch,
        compiler_params=pltpu.CompilerParams(
            collective_id=0, has_side_effects=True, vmem_limit_bytes=60 * 2**20
        ),
    )(passage_lists, slot_map, rec_pos, fresh_q, fresh_kv, pool_kv, jnp.asarray(angle_table()))
    return output, deviation.reshape(ROWS)


def solution(mesh):
    in_specs = (
        P("pool", "ctx"),
        P("pool", "ctx"),
        P(None, "pool", "ctx"),
        P(),
        P(),
        P("pool", None),
    )
    out_specs = (P("pool", "ctx"), P("pool"))
    return jax.shard_map(
        on_device, mesh=mesh, in_specs=in_specs, out_specs=out_specs, check_vma=False
    )
```

```python
import math

import jax
import jax.numpy as jnp
import numpy as np
from jax import lax
from jax.experimental import pallas as pl
from jax.experimental.pallas import tpu as pltpu
from jax.sharding import PartitionSpec as P

HEADS = 64
KVH = 8
HD = 128
PASSAGE = 512
BLOCK_PASSAGES = 2
SEQ_BLOCKS = 16
ROWS = 64
REQS = 4
CTX = 8
SPAN = BLOCK_PASSAGES * PASSAGE
BASE = 500000.0

MESH = pl.DeviceIdType.MESH
F32 = jnp.float32
BF16 = jnp.bfloat16
LOG2_SCALE = math.log2(math.e) / math.sqrt(HD)
NEG = -1e30
FAR = 1 << 30
WIDE = 4 * HD
PIECE = 4
GROUP = 4
STEPS = 4


def frequency_table():
    exponent = np.arange(HD // 2, dtype=np.float32) * np.float32(-2.0 * math.log(BASE) / HD)
    return np.exp(exponent.astype(np.float64)).astype(np.float32)


def angle_table():
    freq = frequency_table()
    offsets = np.arange(SEQ_BLOCKS * BLOCK_PASSAGES).astype(np.float32) * np.float32(PASSAGE)
    angles = (offsets[:, None] * freq[None, :]).astype(np.float64)
    cosine, sine = np.cos(angles), np.sin(angles)
    rows = [
        np.concatenate([cosine, cosine], axis=1),
        np.concatenate([-sine, sine], axis=1),
        np.tile(freq, 2)[None, :],
        np.zeros((7, HD)),
    ]
    return np.concatenate(rows, axis=0).astype(np.float32)


def turned(vectors, cosine, signed_sine):
    half = HD // 2
    swapped = jnp.concatenate([vectors[:, half:], vectors[:, :half]], axis=1)
    return vectors * cosine + swapped * signed_sine


def iota(shape, axis):
    return lax.broadcasted_iota(jnp.int32, shape, axis)


def kernel(
    lists_in, slots_in, rec_in, q_in, fkv_in, pool_in, table_in,
    out_ref, dev_ref,
    lists, slots, rec_ref, q_ref, fkv_ref, pool_ref, table,
    pack, kvb, vt, kpos, fkv, fkv_next, vtf, fpos, recs, qown, qbuf,
    kf_own, meta, sbuf, part, pstat, osend, ssend, orecv, srecv, dsend, drecv, cbuf, xbuf,
    ready, ready_4, ready_8, in_s, kv_ss, kv_rs, rec_ss, rec_rs, f_ss, f_rs, q_ss, q_rs, m_ss, m_rs,
    o_ss, o_rs, s_ss, s_rs, d_ss, d_rs, c_ss, c_rs, x_ss, x_rs,
):
    where = lax.axis_index("pool")
    me_ctx = lax.axis_index("ctx")
    y = where >> 4
    z = where & (SEQ_BLOCKS - 1)

    def node(row, column):
        return {"pool": ((row & (REQS - 1)) << 4) + ((column + SEQ_BLOCKS) & (SEQ_BLOCKS - 1))}

    def remote(src, dst, send, recv, target):
        return pltpu.make_async_remote_copy(
            src_ref=src, dst_ref=dst, send_sem=send, recv_sem=recv,
            device_id=target, device_id_type=MESH,
        )

    inputs = [
        pltpu.make_async_copy(src, dst, in_s.at[i])
        for i, (src, dst) in enumerate(
            [
                (q_in, q_ref), (rec_in, rec_ref), (table_in, table), (fkv_in, fkv_ref),
                (lists_in, lists), (slots_in, slots), (pool_in, pool_ref),
            ]
        )
    ]
    for copy in inputs:
        copy.start()

    barrier = pltpu.get_barrier_semaphore()

    def greet(target):
        pl.semaphore_signal(barrier, inc=1, device_id=target, device_id_type=MESH)

    chips = CTX // 2
    core, chip = me_ctx & 1, me_ctx >> 1

    def same_core(k):
        return ((chip + k) & (chips - 1)) * 2 + core

    for k in (-2, -1, 1, 2):
        greet(node(y, z + k))
    for row in range(1, REQS):
        greet(node(y + row, z))
    greet({"ctx": me_ctx + 1 - 2 * core})
    for k in range(1, chips):
        greet({"ctx": same_core(k)})

    for copy in inputs[:4]:
        copy.wait()
    rec_row = rec_ref[...]
    rec_pair = jnp.concatenate([rec_row, rec_row], axis=1)
    recs[z, 0] = rec_pair
    diagonal = iota((HD, HD), 0) == iota((HD, HD), 1)

    def as_column(row):
        wide = jnp.broadcast_to(row.astype(F32), (HD, HD))
        return jnp.sum(jnp.where(diagonal, wide, 0.0), axis=1, keepdims=True)

    rows_at = as_column(rec_pair)[:ROWS] + (z * SPAN).astype(F32)
    angles = rows_at * table[64:65, :]
    cosine = jnp.cos(angles)
    sine = jnp.sin(angles)
    sine = jnp.where(iota((ROWS, HD), 1) < HD // 2, -sine, sine)
    for pair in range(4):
        both = [
            turned(q_ref[:, (2 * pair + i) * HD : (2 * pair + i + 1) * HD].astype(F32), cosine, sine)
            for i in range(2)
        ]
        stacked = jnp.concatenate(both, axis=0)
        qown[pair] = stacked.T.astype(BF16)
    fresh_key = turned(fkv_ref[:, :HD].astype(F32), cosine, sine).astype(BF16)
    kf_own[...] = fresh_key
    fkv[:, :HD] = fresh_key
    fkv[:, HD:] = fkv_ref[:, HD:]
    for copy in inputs[4:]:
        copy.wait()

    def pack_for(request):
        @pl.loop(0, SEQ_BLOCKS, unroll=16)
        def _(block):
            keys, values = [], []
            for p in range(BLOCK_PASSAGES):
                passage = block * BLOCK_PASSAGES + p
                stored = pool_ref[slots[lists[request, passage]]]
                keys.append(
                    turned(
                        stored[:, :HD].astype(F32),
                        table[pl.ds(passage, 1), :],
                        table[pl.ds(passage + 32, 1), :],
                    )
                )
                values.append(stored[:, HD:].astype(F32))
            pack[request, block, :, :HD] = jnp.concatenate(keys, axis=0).astype(BF16)
            pack[request, block, :, HD:] = jnp.concatenate(values, axis=0).astype(BF16)

    for step in range(REQS):
        pack_for(step)

    pl.semaphore_wait(barrier, 4 + (REQS - 1) + 1 + chips - 1)
    for row in range(1, REQS):
        pl.semaphore_signal(ready, inc=1, device_id=node(y + row, z), device_id_type=MESH)
    for k in (-2, 2):
        pl.semaphore_signal(ready_4, inc=1, device_id=node(y, z + k), device_id_type=MESH)

    def along(d):
        return node(y, z + (2 - 4 * d))

    def q_copy(d, s, c):
        src = qown.at[c] if s == 0 else qbuf.at[d, s - 1, c]
        return remote(src, qbuf.at[d, s, c], q_ss.at[d, s, c], q_rs.at[d, s, c], along(d))

    def in_turn(first=0, count=4):
        return [((k + 2 * d) % 4, d) for k in range(first, first + count) for d in range(2)]

    def meta_copy(d, s):
        src = kf_own if s == 0 else meta.at[d, s - 1]
        return remote(src, meta.at[d, s], m_ss.at[d, s], m_rs.at[d, s], along(d))

    def side(row_a, row_b):
        return ((row_a + row_b) & 2) - 1

    def kv_copy(i, step, first=0, count=SEQ_BLOCKS):
        row = (y + step) & (REQS - 1)
        shift = side(y, row) if i else 0
        slot = i * REQS + y
        blocks = pl.ds(first, count)
        return remote(
            pack.at[row, blocks], kvb.at[blocks, slot], kv_ss.at[i, step], kv_rs.at[slot],
            node(row, z + shift),
        )

    def next_copy():
        return remote(
            recs.at[z, 0], recs.at[(z - 1) & (SEQ_BLOCKS - 1), 1], rec_ss.at[0], rec_rs.at[SEQ_BLOCKS],
            node(y, z - 1),
        )

    def next_wait():
        remote(
            recs.at[z, 0], recs.at[z, 1], rec_ss.at[0], rec_rs.at[SEQ_BLOCKS], node(y, z - 1)
        ).wait_recv()

    def rec_copy(k):
        return remote(recs.at[z], recs.at[z], rec_ss.at[k], rec_rs.at[z], node(y, z + 2 * k))

    def positions(tile):
        odd = (tile ^ z) & 1
        return recs[(tile - odd) & (SEQ_BLOCKS - 1), odd]

    def fresh_copy():
        return remote(fkv, fkv_next, f_ss.at[0], f_rs.at[0], node(y, z + 1))

    def stat_copy(d, s, h):
        return remote(
            ssend.at[d, s, h], srecv.at[d, s, h], s_ss.at[d, s, h], s_rs.at[d, s, h], along(1 - d)
        )

    def out_copy(d, s, c):
        return remote(
            osend.at[d, s, c], orecv.at[d, s, c], o_ss.at[d, s, c], o_rs.at[d, s, c], along(1 - d)
        )

    def dev_copy(k):
        return remote(dsend.at[k], drecv.at[k], d_ss.at[k], d_rs.at[k], node(y, z - 2 * k))

    def core_copy():
        return remote(cbuf.at[0], cbuf.at[1], c_ss.at[0], c_rs.at[0], {"ctx": me_ctx + 1 - 2 * core})

    def chip_copy(k):
        return remote(
            xbuf.at[chip], xbuf.at[chip], x_ss.at[k], x_rs.at[chip], {"ctx": same_core(k)}
        )

    def q_on(d, s, c):
        q_copy(d, s, c).wait_recv()
        if s < STEPS - 2 or (s == STEPS - 2 and c // 2 == d):
            q_copy(d, s + 1, c).start()

    def meta_on(d, s):
        meta_copy(d, s).wait_recv()
        if s < STEPS - 2 or (s == STEPS - 2 and d == 0):
            meta_copy(d, s + 1).start()

    own_kv = pltpu.make_async_copy(pack.at[y], kvb.at[:, y], kv_rs.at[y])
    next_copy().start()
    for c, d in in_turn(0, 2):
        q_copy(d, 0, c).start()
    own_kv.start()

    def kv_piece(i, n):
        for step in (2, 1, 3, 0):
            if i or step:
                kv_copy(i, step, n * PIECE, PIECE).start()

    kv_piece(0, 0)
    for c, d in in_turn(2, 1):
        q_copy(d, 0, c).start()
    pl.semaphore_wait(ready, REQS - 1)
    kv_piece(1, 0)
    for c, d in in_turn(3, 1):
        q_copy(d, 0, c).start()
    pl.semaphore_wait(ready_4, 2)
    for k in (-4, 4):
        pl.semaphore_signal(ready_8, inc=1, device_id=node(y, z + k), device_id_type=MESH)
    for i in range(2):
        kv_piece(i, 1)
    for d in range(2):
        meta_copy(d, 0).start()
    fresh_copy().start()
    for c, d in in_turn(0, 2):
        q_on(d, 0, c)
    pl.semaphore_wait(ready_8, 2)
    next_wait()
    for k in (4, 3, 5, 2, 6, 1, 7):
        rec_copy(k).start()
    for i in range(2):
        kv_piece(i, 2)
    for c, d in in_turn(2, 2):
        q_on(d, 0, c)
    for i in range(2):
        kv_piece(i, 3)
    for d in range(2):
        meta_on(d, 0)

    key = iota((HD, HD), 0)
    key_row = (key >> 4) & 3
    key_side = ((y + key_row) & 3) & 2
    key_column = (z - (key >> 6) * (key_side - 1) + SEQ_BLOCKS) & (SEQ_BLOCKS - 1)
    offset = ((key >> 3) & 1) * PASSAGE + key_row * 128 + key_column * 8 + (key & 7)

    def tile_of(d, s):
        return (z - (2 - 4 * d) * (s + 1) + SEQ_BLOCKS) & (SEQ_BLOCKS - 1)

    def far_on(s):
        for c, d in in_turn(0, 2):
            q_on(d, s, c)

    def near_on(s):
        for c, d in in_turn(2, 2):
            q_on(d, s, c)
        for d in range(2):
            meta_on(d, s)

    far_on(1)
    for k in range(1, 8):
        other = (z + 2 * k) & (SEQ_BLOCKS - 1)
        remote(
            recs.at[z], recs.at[other], rec_ss.at[k], rec_rs.at[other], node(y, z + 2 * k)
        ).wait_recv()

    @pl.loop(0, SEQ_BLOCKS, unroll=2)
    def _(block):
        same = jnp.where(offset == positions(block), 1.0, 0.0)
        replaced = jnp.max(same, axis=1, keepdims=True) > 0.0
        kpos[block] = jnp.where(replaced, FAR, offset + block * SPAN)

    before = (z + SEQ_BLOCKS - 1) & (SEQ_BLOCKS - 1)
    fresh_row = jnp.where(
        iota((1, HD), 1) < ROWS, positions(z) + z * SPAN, positions(before) + before * SPAN
    )
    fpos[...] = jnp.broadcast_to(as_column(fresh_row), (HD, HD)).astype(jnp.int32)

    near_on(1)

    for slot in range(2 * REQS):
        pltpu.make_async_copy(pack.at[0], kvb.at[:, slot], kv_rs.at[slot]).wait()
    fresh_copy().wait_recv()

    @pl.loop(0, SEQ_BLOCKS // GROUP)
    def _(g):
        for i in range(GROUP):
            values = kvb[pl.ds(GROUP * g + i, 1), :, :, HD:].reshape(HD, HD)
            vt[g, :, i * HD : (i + 1) * HD] = values.astype(F32).T.astype(BF16)

    fresh_values = jnp.concatenate([fkv[:, HD:], fkv_next[:, HD:]], axis=0)
    vtf[...] = fresh_values.astype(F32).T.astype(BF16)

    halves = [slice(0, 2 * HD), slice(2 * HD, 4 * HD)]

    def score(query, at, blocks, columns):
        top = None
        for i, (keys, places) in enumerate(blocks):
            seen = places <= at
            scores = jnp.dot(keys, query[:, columns], preferred_element_type=F32)
            scores = jnp.where(jnp.concatenate([seen, seen], axis=1), scores, NEG)
            sbuf[i, :, columns] = scores
            largest = jnp.max(scores.reshape(HD // 8, 8, 2 * HD), axis=0)
            top = largest if top is None else jnp.maximum(top, largest)
        return jnp.max(top, axis=0, keepdims=True)

    def weigh(top, groups, columns):
        total, acc = None, None
        for members, values_t in groups:
            rounded = []
            for i in members:
                weights = jnp.exp2((sbuf[i, :, columns] - top) * LOG2_SCALE)
                summed = jnp.sum(weights.reshape(HD // 8, 8, 2 * HD), axis=0)
                total = summed if total is None else total + summed
                rounded.append(weights.astype(BF16))
            product = jnp.dot(
                values_t, jnp.concatenate(rounded, axis=0), preferred_element_type=F32
            )
            acc = product if acc is None else acc + product
        return jnp.sum(total, axis=0, keepdims=True), acc

    def stored(g):
        return [
            (kvb[g * GROUP + i, :, :, :HD].reshape(HD, HD), kpos[g * GROUP + i])
            for i in range(GROUP)
        ]

    def attend(tile, queries, job):
        at = positions(tile) + tile * SPAN
        query = jnp.concatenate([one[...] for one in queries], axis=1)
        fresh_keys = jnp.concatenate([fkv[:, :HD], fkv_next[:, :HD]], axis=0)
        blocks = [(fresh_keys, fpos[...])] + stored(0)
        groups = [([0], vtf[...]), (list(range(1, GROUP + 1)), vt[0])]
        tops = [score(query, at, blocks, columns) for columns in halves]
        for columns, top in zip(halves, tops):
            total, acc = weigh(top, groups, columns)
            part[job, :, columns] = acc
            pstat[job, 0:1, columns] = top
            pstat[job, 1:2, columns] = total

        @pl.loop(1, (tile >> 2) + 1)
        def _(g):
            groups = [(list(range(GROUP)), vt[g])]
            tops = [score(query, at, stored(g), columns) for columns in halves]
            for columns, top in zip(halves, tops):
                old_top = pstat[job, 0:1, columns]
                top = jnp.maximum(old_top, top)
                total, acc = weigh(top, groups, columns)
                factor = jnp.exp2((old_top - top) * LOG2_SCALE)
                part[job, :, columns] = part[job, :, columns] * factor + acc
                pstat[job, 0:1, columns] = top
                pstat[job, 1:2, columns] = pstat[job, 1:2, columns] * factor + total

    def job_of(d, s):
        return 7 if s == STEPS - 1 else 1 + 2 * s + d

    def jobs(s):
        @pl.loop(0, 2)
        def _(d):
            attend(tile_of(d, s), [qbuf.at[d, s, c] for c in range(4)], 1 + 2 * s + d)

    def gap_of(tile, keys, k):
        same = jnp.where(offset == positions(tile), 1.0, 0.0)[:, :ROWS].astype(BF16)
        cached = kvb[pl.ds(tile, 1), :, :, :HD].reshape(HD, HD)
        over = (((0,), (0,)), ((), ()))
        found = lax.dot_general(same, cached, over, preferred_element_type=F32)
        hit = lax.dot_general(same, jnp.ones((HD, HD), BF16), over, preferred_element_type=F32)
        gap = (found - keys.astype(F32)) * hit
        squares = (gap * gap).T
        dsend[k, :, :ROWS] = jnp.sum(squares, axis=0, keepdims=True)

    def stats_of(job, h):
        columns = slice(h * 2 * HD, (h + 1) * 2 * HD)
        return pstat[job, 0:1, columns], pstat[job, 1:2, columns]

    def part_of(job, c):
        return part[job, :, c * HD : (c + 1) * HD]

    def combine(d, s, h, job):
        top, total = stats_of(job, h)
        stat_copy(d, s, h).wait_recv()
        other = srecv[d, s, h]
        other_top = jnp.concatenate([other[0:1, :], other[1:2, :]], axis=1)
        other_total = jnp.concatenate([other[2:3, :], other[3:4, :]], axis=1)
        new_top = jnp.maximum(top, other_top)
        mine = jnp.exp2((top - new_top) * LOG2_SCALE)
        theirs = jnp.exp2((other_top - new_top) * LOG2_SCALE)
        return new_top, total * mine + other_total * theirs, mine, theirs

    def summed(d, s, h, i, job, mine, theirs):
        columns = slice(i * HD, (i + 1) * HD)
        out_copy(d, s, 2 * h + i).wait_recv()
        far = orecv[d, s, 2 * h + i].astype(F32)
        return part_of(job, 2 * h + i) * mine[:, columns] + far * theirs[:, columns]

    def hand_on(s, furthest):
        first = s == STEPS - 1 or (s == STEPS - 2 and not furthest)
        factors = []
        for d in range(2):
            h = d if furthest else 1 - d
            job = job_of(d, s)
            if first:
                top, total = stats_of(job, h)
                factors.append(None)
            else:
                top, total, mine, theirs = combine(d, s + 1, h, job)
                factors.append((mine, theirs))
            ssend[d, s, h, 0:1, :] = top[:, :HD]
            ssend[d, s, h, 1:2, :] = top[:, HD:]
            ssend[d, s, h, 2:3, :] = total[:, :HD]
            ssend[d, s, h, 3:4, :] = total[:, HD:]
            stat_copy(d, s, h).start()
        for i in range(2):
            for d in range(2):
                h = d if furthest else 1 - d
                job = job_of(d, s)
                if first:
                    acc = part_of(job, 2 * h + i)
                else:
                    acc = summed(d, s + 1, h, i, job, *factors[d])
                osend[d, s, 2 * h + i] = acc.astype(BF16)
                out_copy(d, s, 2 * h + i).start()

    def gaps(s):
        for d in range(2 if s < STEPS - 1 else 1):
            k = s + 1 if d == 0 else SEQ_BLOCKS // 2 - s - 1
            gap_of(tile_of(d, s), meta[d, s], k)
            dev_copy(k).start()

    dsend[...] = jnp.zeros_like(dsend)
    far_on(2)
    attend(z, [qown.at[c] for c in range(4)], 0)
    near_on(2)
    jobs(2)
    hand_on(2, False)
    for c, d in in_turn(0, 2):
        q_copy(d, 3, c).wait_recv()
    attend(tile_of(0, 3), [qbuf.at[c // 2, 3, c] for c in range(4)], 7)
    hand_on(3, True)
    jobs(1)
    hand_on(1, False)
    meta_copy(0, 3).wait_recv()
    gaps(3)
    gaps(2)
    hand_on(2, True)
    jobs(0)
    hand_on(0, False)
    gaps(1)
    gaps(0)
    gap_of(z, fkv[:, :HD], 0)
    hand_on(1, True)
    for k in range(1, 8):
        dev_copy(k).wait_recv()
    shared = dsend[0]
    for k in range(1, 8):
        shared = shared + drecv[k]
    cbuf[0] = shared
    core_copy().start()
    hand_on(0, True)
    core_copy().wait_recv()
    xbuf[chip] = cbuf[0] + cbuf[1]
    for k in range(1, chips):
        chip_copy(k).start()

    def home(d, h):
        top, total, mine, theirs = combine(d, 0, h, 0)
        columns = slice(h * 2 * HD, (h + 1) * 2 * HD)
        pstat[0, 0:1, columns] = top
        pstat[0, 1:2, columns] = total
        for i in range(2):
            acc = summed(d, 0, h, i, 0, mine, theirs)
            part[0, :, (2 * h + i) * HD : (2 * h + i + 1) * HD] = acc

    for h in range(2):
        home(1 - h, h)
    for k in range(1, chips):
        other = (chip + k) & (chips - 1)
        remote(
            xbuf.at[chip], xbuf.at[other], x_ss.at[k], x_rs.at[other], {"ctx": same_core(k)}
        ).wait_recv()
    gathered = xbuf[0]
    for k in range(1, chips):
        gathered = gathered + xbuf[k]
    dev_ref[...] = gathered[:, :ROWS] / (KVH * HD)

    for h in range(2):
        home(h, h)
        for pair in range(2):
            columns = slice((2 * h + pair) * HD, (2 * h + pair + 1) * HD)
            upright = (part[0, :, columns] / pstat[0, 1:2, columns]).T.astype(BF16)
            for i in range(2):
                head = h * 4 + pair * 2 + i
                out_ref[:, head * HD : (head + 1) * HD] = upright[i * ROWS : (i + 1) * ROWS]

    next_copy().wait_send()
    for k in range(1, 8):
        rec_copy(k).wait_send()
        dev_copy(k).wait_send()
    for step in range(REQS):
        if step:
            kv_copy(0, step).wait_send()
        kv_copy(1, step).wait_send()
    fresh_copy().wait_send()
    for d in range(2):
        for s in range(STEPS):
            for c in range(4):
                if s < STEPS - 1 or c // 2 == d:
                    q_copy(d, s, c).wait_send()
                    out_copy(d, s, c).wait_send()
                    if c % 2 == 0:
                        stat_copy(d, s, c // 2).wait_send()
            if s < STEPS - 1 or d == 0:
                meta_copy(d, s).wait_send()
    core_copy().wait_send()
    for k in range(1, chips):
        chip_copy(k).wait_send()


def on_device(fresh_q, fresh_kv, pool_kv, passage_lists, slot_map, rec_pos):
    vmem = pl.BlockSpec(memory_space=pltpu.VMEM)
    anywhere = pl.BlockSpec(memory_space=pl.ANY)
    dma = pltpu.SemaphoreType.DMA
    scratch = [
        pltpu.SMEM(passage_lists.shape, jnp.int32),
        pltpu.SMEM(slot_map.shape, jnp.int32),
        pltpu.VMEM(rec_pos.shape, jnp.int32),
        pltpu.VMEM(fresh_q.shape, BF16),
        pltpu.VMEM(fresh_kv.shape, BF16),
        pltpu.VMEM(pool_kv.shape, BF16),
        pltpu.VMEM((72, HD), F32),
        pltpu.VMEM((REQS, SEQ_BLOCKS, 16, 2 * HD), BF16),
        pltpu.VMEM((SEQ_BLOCKS, 2 * REQS, 16, 2 * HD), BF16),
        pltpu.VMEM((SEQ_BLOCKS // GROUP, HD, GROUP * HD), BF16),
        pltpu.VMEM((SEQ_BLOCKS, HD, HD), jnp.int32),
        pltpu.VMEM((ROWS, 2 * HD), BF16),
        pltpu.VMEM((ROWS, 2 * HD), BF16),
        pltpu.VMEM((HD, HD), BF16),
        pltpu.VMEM((HD, HD), jnp.int32),
        pltpu.VMEM((SEQ_BLOCKS, 2, 1, HD), jnp.int32),
        pltpu.VMEM((4, HD, HD), BF16),
        pltpu.VMEM((2, STEPS, 4, HD, HD), BF16),
        pltpu.VMEM((ROWS, HD), BF16),
        pltpu.VMEM((2, STEPS, ROWS, HD), BF16),
        pltpu.VMEM((GROUP + 1, HD, WIDE), F32),
        pltpu.VMEM((8, HD, WIDE), F32),
        pltpu.VMEM((8, 8, WIDE), F32),
        pltpu.VMEM((2, STEPS, 4, HD, HD), BF16),
        pltpu.VMEM((2, STEPS, 2, 4, HD), F32),
        pltpu.VMEM((2, STEPS, 4, HD, HD), BF16),
        pltpu.VMEM((2, STEPS, 2, 4, HD), F32),
        pltpu.VMEM((8, 1, HD), F32),
        pltpu.VMEM((8, 1, HD), F32),
        pltpu.VMEM((2, 1, HD), F32),
        pltpu.VMEM((CTX // 2, 1, HD), F32),
        pltpu.SemaphoreType.REGULAR,
        pltpu.SemaphoreType.REGULAR,
        pltpu.SemaphoreType.REGULAR,
        dma((7,)),
        dma((2, REQS)), dma((2 * REQS,)),
        dma((SEQ_BLOCKS,)), dma((SEQ_BLOCKS + 1,)),
        dma((1,)), dma((1,)),
        dma((2, STEPS, 4)), dma((2, STEPS, 4)),
        dma((2, STEPS)), dma((2, STEPS)),
        dma((2, STEPS, 4)), dma((2, STEPS, 4)),
        dma((2, STEPS, 2)), dma((2, STEPS, 2)),
        dma((8,)), dma((8,)),
        dma((1,)), dma((1,)),
        dma((CTX // 2,)), dma((CTX // 2,)),
    ]
    output, deviation = pl.pallas_call(
        kernel,
        out_shape=(
            jax.ShapeDtypeStruct((ROWS, HEADS // CTX * HD), BF16),
            jax.ShapeDtypeStruct((1, ROWS), F32),
        ),
        in_specs=[anywhere] * 7,
        out_specs=(vmem, vmem),
        scratch_shapes=scratch,
        compiler_params=pltpu.CompilerParams(
            collective_id=0, has_side_effects=True, vmem_limit_bytes=60 * 2**20
        ),
    )(passage_lists, slot_map, rec_pos, fresh_q, fresh_kv, pool_kv, jnp.asarray(angle_table()))
    return output, deviation.reshape(ROWS)


def solution(mesh):
    in_specs = (
        P("pool", "ctx"),
        P("pool", "ctx"),
        P(None, "pool", "ctx"),
        P(),
        P(),
        P("pool", None),
    )
    out_specs = (P("pool", "ctx"), P("pool"))
    return jax.shard_map(
        on_device, mesh=mesh, in_specs=in_specs, out_specs=out_specs, check_vma=False
    )
```

```python
import math

import jax
import jax.numpy as jnp
import numpy as np
from jax import lax
from jax.experimental import pallas as pl
from jax.experimental.pallas import tpu as pltpu
from jax.sharding import PartitionSpec as P

HEADS = 64
KVH = 8
HD = 128
PASSAGE = 512
BLOCK_PASSAGES = 2
SEQ_BLOCKS = 16
ROWS = 64
REQS = 4
CTX = 8
SPAN = BLOCK_PASSAGES * PASSAGE
BASE = 500000.0

MESH = pl.DeviceIdType.MESH
F32 = jnp.float32
BF16 = jnp.bfloat16
LOG2_SCALE = math.log2(math.e) / math.sqrt(HD)
NEG = -1e30
FAR = 1 << 30
WIDE = 4 * HD
PIECE = 4
GROUP = 4
STEPS = 4


def frequency_table():
    exponent = np.arange(HD // 2, dtype=np.float32) * np.float32(-2.0 * math.log(BASE) / HD)
    return np.exp(exponent.astype(np.float64)).astype(np.float32)


def angle_table():
    freq = frequency_table()
    offsets = np.arange(SEQ_BLOCKS * BLOCK_PASSAGES).astype(np.float32) * np.float32(PASSAGE)
    angles = (offsets[:, None] * freq[None, :]).astype(np.float64)
    cosine, sine = np.cos(angles), np.sin(angles)
    rows = [
        np.concatenate([cosine, cosine], axis=1),
        np.concatenate([-sine, sine], axis=1),
        np.tile(freq, 2)[None, :],
        np.zeros((7, HD)),
    ]
    return np.concatenate(rows, axis=0).astype(np.float32)


def turned(vectors, cosine, signed_sine):
    half = HD // 2
    swapped = jnp.concatenate([vectors[:, half:], vectors[:, :half]], axis=1)
    return vectors * cosine + swapped * signed_sine


def iota(shape, axis):
    return lax.broadcasted_iota(jnp.int32, shape, axis)


def kernel(
    lists_in, slots_in, rec_in, q_in, fkv_in, pool_in, table_in,
    out_ref, dev_ref,
    lists, slots, rec_ref, q_ref, fkv_ref, pool_ref, table,
    pack, kvb, vt, kpos, fkv, fkv_next, vtf, fpos, recs, qown, qbuf,
    out_buf, kf_own, meta, sbuf, part, pstat, osend, ssend, orecv, srecv, dsend, drecv, cbuf, xbuf,
    ready, ready_4, ready_8, out_s, in_s, kv_ss, kv_rs, rec_ss, rec_rs, f_ss, f_rs, q_ss, q_rs, m_ss, m_rs,
    o_ss, o_rs, s_ss, s_rs, d_ss, d_rs, c_ss, c_rs, x_ss, x_rs,
):
    where = lax.axis_index("pool")
    me_ctx = lax.axis_index("ctx")
    y = where >> 4
    z = where & (SEQ_BLOCKS - 1)

    def node(row, column):
        return {"pool": ((row & (REQS - 1)) << 4) + ((column + SEQ_BLOCKS) & (SEQ_BLOCKS - 1))}

    def remote(src, dst, send, recv, target):
        return pltpu.make_async_remote_copy(
            src_ref=src, dst_ref=dst, send_sem=send, recv_sem=recv,
            device_id=target, device_id_type=MESH,
        )

    inputs = [
        pltpu.make_async_copy(src, dst, in_s.at[i])
        for i, (src, dst) in enumerate(
            [
                (q_in, q_ref), (rec_in, rec_ref), (table_in, table), (fkv_in, fkv_ref),
                (lists_in, lists), (slots_in, slots), (pool_in, pool_ref),
            ]
        )
    ]
    for copy in inputs:
        copy.start()

    barrier = pltpu.get_barrier_semaphore()

    def greet(target):
        pl.semaphore_signal(barrier, inc=1, device_id=target, device_id_type=MESH)

    chips = CTX // 2
    core, chip = me_ctx & 1, me_ctx >> 1

    def same_core(k):
        return ((chip + k) & (chips - 1)) * 2 + core

    for k in (-2, -1, 1, 2):
        greet(node(y, z + k))
    for row in range(1, REQS):
        greet(node(y + row, z))
    greet({"ctx": me_ctx + 1 - 2 * core})
    for k in range(1, chips):
        greet({"ctx": same_core(k)})

    for copy in inputs[:4]:
        copy.wait()
    rec_row = rec_ref[...]
    rec_pair = jnp.concatenate([rec_row, rec_row], axis=1)
    recs[z, 0] = rec_pair
    diagonal = iota((HD, HD), 0) == iota((HD, HD), 1)

    def as_column(row):
        wide = jnp.broadcast_to(row.astype(F32), (HD, HD))
        return jnp.sum(jnp.where(diagonal, wide, 0.0), axis=1, keepdims=True)

    rows_at = as_column(rec_pair)[:ROWS] + (z * SPAN).astype(F32)
    angles = rows_at * table[64:65, :]
    cosine = jnp.cos(angles)
    sine = jnp.sin(angles)
    sine = jnp.where(iota((ROWS, HD), 1) < HD // 2, -sine, sine)
    for pair in range(4):
        both = [
            turned(q_ref[:, (2 * pair + i) * HD : (2 * pair + i + 1) * HD].astype(F32), cosine, sine)
            for i in range(2)
        ]
        stacked = jnp.concatenate(both, axis=0)
        qown[pair] = stacked.T.astype(BF16)
    fresh_key = turned(fkv_ref[:, :HD].astype(F32), cosine, sine).astype(BF16)
    kf_own[...] = fresh_key
    fkv[:, :HD] = fresh_key
    fkv[:, HD:] = fkv_ref[:, HD:]
    for copy in inputs[4:]:
        copy.wait()

    def pack_for(request):
        @pl.loop(0, SEQ_BLOCKS, unroll=16)
        def _(block):
            keys, values = [], []
            for p in range(BLOCK_PASSAGES):
                passage = block * BLOCK_PASSAGES + p
                stored = pool_ref[slots[lists[request, passage]]]
                keys.append(
                    turned(
                        stored[:, :HD].astype(F32),
                        table[pl.ds(passage, 1), :],
                        table[pl.ds(passage + 32, 1), :],
                    )
                )
                values.append(stored[:, HD:].astype(F32))
            pack[request, block, :, :HD] = jnp.concatenate(keys, axis=0).astype(BF16)
            pack[request, block, :, HD:] = jnp.concatenate(values, axis=0).astype(BF16)

    for step in range(REQS):
        pack_for(step)

    pl.semaphore_wait(barrier, 4 + (REQS - 1) + 1 + chips - 1)
    for row in range(1, REQS):
        pl.semaphore_signal(ready, inc=1, device_id=node(y + row, z), device_id_type=MESH)
    for k in (-2, 2):
        pl.semaphore_signal(ready_4, inc=1, device_id=node(y, z + k), device_id_type=MESH)

    def along(d):
        return node(y, z + (2 - 4 * d))

    def q_copy(d, s, c):
        src = qown.at[c] if s == 0 else qbuf.at[d, s - 1, c]
        return remote(src, qbuf.at[d, s, c], q_ss.at[d, s, c], q_rs.at[d, s, c], along(d))

    def in_turn(first=0, count=4):
        return [((k + 2 * d) % 4, d) for k in range(first, first + count) for d in range(2)]

    def meta_copy(d, s):
        src = kf_own if s == 0 else meta.at[d, s - 1]
        return remote(src, meta.at[d, s], m_ss.at[d, s], m_rs.at[d, s], along(d))

    def side(row_a, row_b):
        return ((row_a + row_b) & 2) - 1

    def kv_copy(i, step, first=0, count=SEQ_BLOCKS):
        row = (y + step) & (REQS - 1)
        shift = side(y, row) if i else 0
        slot = i * REQS + y
        blocks = pl.ds(first, count)
        return remote(
            pack.at[row, blocks], kvb.at[blocks, slot], kv_ss.at[i, step], kv_rs.at[slot],
            node(row, z + shift),
        )

    def next_copy():
        return remote(
            recs.at[z, 0], recs.at[(z - 1) & (SEQ_BLOCKS - 1), 1], rec_ss.at[0], rec_rs.at[SEQ_BLOCKS],
            node(y, z - 1),
        )

    def next_wait():
        remote(
            recs.at[z, 0], recs.at[z, 1], rec_ss.at[0], rec_rs.at[SEQ_BLOCKS], node(y, z - 1)
        ).wait_recv()

    def rec_copy(k):
        return remote(recs.at[z], recs.at[z], rec_ss.at[k], rec_rs.at[z], node(y, z + 2 * k))

    def positions(tile):
        odd = (tile ^ z) & 1
        return recs[(tile - odd) & (SEQ_BLOCKS - 1), odd]

    def fresh_copy():
        return remote(fkv, fkv_next, f_ss.at[0], f_rs.at[0], node(y, z + 1))

    def stat_copy(d, s, h):
        return remote(
            ssend.at[d, s, h], srecv.at[d, s, h], s_ss.at[d, s, h], s_rs.at[d, s, h], along(1 - d)
        )

    def out_copy(d, s, c):
        return remote(
            osend.at[d, s, c], orecv.at[d, s, c], o_ss.at[d, s, c], o_rs.at[d, s, c], along(1 - d)
        )

    def dev_copy(k):
        return remote(dsend.at[k], drecv.at[k], d_ss.at[k], d_rs.at[k], node(y, z - 2 * k))

    def core_copy():
        return remote(cbuf.at[0], cbuf.at[1], c_ss.at[0], c_rs.at[0], {"ctx": me_ctx + 1 - 2 * core})

    def chip_copy(k):
        return remote(
            xbuf.at[chip], xbuf.at[chip], x_ss.at[k], x_rs.at[chip], {"ctx": same_core(k)}
        )

    def q_on(d, s, c):
        q_copy(d, s, c).wait_recv()
        if s < STEPS - 2 or (s == STEPS - 2 and c // 2 == d):
            q_copy(d, s + 1, c).start()

    def meta_on(d, s):
        meta_copy(d, s).wait_recv()
        if s < STEPS - 2 or (s == STEPS - 2 and d == 0):
            meta_copy(d, s + 1).start()

    own_kv = pltpu.make_async_copy(pack.at[y], kvb.at[:, y], kv_rs.at[y])
    next_copy().start()
    for c, d in in_turn(0, 2):
        q_copy(d, 0, c).start()
    own_kv.start()

    def kv_piece(i, n):
        for step in (2, 1, 3, 0):
            if i or step:
                kv_copy(i, step, n * PIECE, PIECE).start()

    kv_piece(0, 0)
    for c, d in in_turn(2, 1):
        q_copy(d, 0, c).start()
    pl.semaphore_wait(ready, REQS - 1)
    kv_piece(1, 0)
    for c, d in in_turn(3, 1):
        q_copy(d, 0, c).start()
    pl.semaphore_wait(ready_4, 2)
    for k in (-4, 4):
        pl.semaphore_signal(ready_8, inc=1, device_id=node(y, z + k), device_id_type=MESH)
    for i in range(2):
        kv_piece(i, 1)
    for d in range(2):
        meta_copy(d, 0).start()
    fresh_copy().start()
    for c, d in in_turn(0, 2):
        q_on(d, 0, c)
    pl.semaphore_wait(ready_8, 2)
    next_wait()
    for k in (4, 3, 5, 2, 6, 1, 7):
        rec_copy(k).start()
    for i in range(2):
        kv_piece(i, 2)
    for c, d in in_turn(2, 2):
        q_on(d, 0, c)
    for i in range(2):
        kv_piece(i, 3)
    for d in range(2):
        meta_on(d, 0)

    key = iota((HD, HD), 0)
    key_row = (key >> 4) & 3
    key_side = ((y + key_row) & 3) & 2
    key_column = (z - (key >> 6) * (key_side - 1) + SEQ_BLOCKS) & (SEQ_BLOCKS - 1)
    offset = ((key >> 3) & 1) * PASSAGE + key_row * 128 + key_column * 8 + (key & 7)

    def tile_of(d, s):
        return (z - (2 - 4 * d) * (s + 1) + SEQ_BLOCKS) & (SEQ_BLOCKS - 1)

    def far_on(s):
        for c, d in in_turn(0, 2):
            q_on(d, s, c)

    def near_on(s):
        for c, d in in_turn(2, 2):
            q_on(d, s, c)
        for d in range(2):
            meta_on(d, s)

    far_on(1)
    for k in range(1, 8):
        other = (z + 2 * k) & (SEQ_BLOCKS - 1)
        remote(
            recs.at[z], recs.at[other], rec_ss.at[k], rec_rs.at[other], node(y, z + 2 * k)
        ).wait_recv()

    @pl.loop(0, SEQ_BLOCKS, unroll=2)
    def _(block):
        same = jnp.where(offset == positions(block), 1.0, 0.0)
        replaced = jnp.max(same, axis=1, keepdims=True) > 0.0
        kpos[block] = jnp.where(replaced, FAR, offset + block * SPAN)

    before = (z + SEQ_BLOCKS - 1) & (SEQ_BLOCKS - 1)
    fresh_row = jnp.where(
        iota((1, HD), 1) < ROWS, positions(z) + z * SPAN, positions(before) + before * SPAN
    )
    fpos[...] = jnp.broadcast_to(as_column(fresh_row), (HD, HD)).astype(jnp.int32)

    near_on(1)

    for slot in range(2 * REQS):
        pltpu.make_async_copy(pack.at[0], kvb.at[:, slot], kv_rs.at[slot]).wait()
    fresh_copy().wait_recv()

    @pl.loop(0, SEQ_BLOCKS // GROUP)
    def _(g):
        for i in range(GROUP):
            values = kvb[pl.ds(GROUP * g + i, 1), :, :, HD:].reshape(HD, HD)
            vt[g, :, i * HD : (i + 1) * HD] = values.astype(F32).T.astype(BF16)

    fresh_values = jnp.concatenate([fkv[:, HD:], fkv_next[:, HD:]], axis=0)
    vtf[...] = fresh_values.astype(F32).T.astype(BF16)

    halves = [slice(0, 2 * HD), slice(2 * HD, 4 * HD)]

    def score(query, at, blocks, columns):
        top = None
        for i, (keys, places) in enumerate(blocks):
            seen = places <= at
            scores = jnp.dot(keys, query[:, columns], preferred_element_type=F32)
            scores = jnp.where(jnp.concatenate([seen, seen], axis=1), scores, NEG)
            sbuf[i, :, columns] = scores
            largest = jnp.max(scores.reshape(HD // 8, 8, 2 * HD), axis=0)
            top = largest if top is None else jnp.maximum(top, largest)
        return jnp.max(top, axis=0, keepdims=True)

    def weigh(top, groups, columns):
        total, acc = None, None
        for members, values_t in groups:
            rounded = []
            for i in members:
                weights = jnp.exp2((sbuf[i, :, columns] - top) * LOG2_SCALE)
                summed = jnp.sum(weights.reshape(HD // 8, 8, 2 * HD), axis=0)
                total = summed if total is None else total + summed
                rounded.append(weights.astype(BF16))
            product = jnp.dot(
                values_t, jnp.concatenate(rounded, axis=0), preferred_element_type=F32
            )
            acc = product if acc is None else acc + product
        return jnp.sum(total, axis=0, keepdims=True), acc

    def stored(g):
        return [
            (kvb[g * GROUP + i, :, :, :HD].reshape(HD, HD), kpos[g * GROUP + i])
            for i in range(GROUP)
        ]

    def attend(tile, queries, job):
        at = positions(tile) + tile * SPAN
        query = jnp.concatenate([one[...] for one in queries], axis=1)
        fresh_keys = jnp.concatenate([fkv[:, :HD], fkv_next[:, :HD]], axis=0)
        blocks = [(fresh_keys, fpos[...])] + stored(0)
        groups = [([0], vtf[...]), (list(range(1, GROUP + 1)), vt[0])]
        tops = [score(query, at, blocks, columns) for columns in halves]
        for columns, top in zip(halves, tops):
            total, acc = weigh(top, groups, columns)
            part[job, :, columns] = acc
            pstat[job, 0:1, columns] = top
            pstat[job, 1:2, columns] = total

        @pl.loop(1, (tile >> 2) + 1)
        def _(g):
            groups = [(list(range(GROUP)), vt[g])]
            tops = [score(query, at, stored(g), columns) for columns in halves]
            for columns, top in zip(halves, tops):
                old_top = pstat[job, 0:1, columns]
                top = jnp.maximum(old_top, top)
                total, acc = weigh(top, groups, columns)
                factor = jnp.exp2((old_top - top) * LOG2_SCALE)
                part[job, :, columns] = part[job, :, columns] * factor + acc
                pstat[job, 0:1, columns] = top
                pstat[job, 1:2, columns] = pstat[job, 1:2, columns] * factor + total

    def job_of(d, s):
        return 7 if s == STEPS - 1 else 1 + 2 * s + d

    def jobs(s):
        @pl.loop(0, 2)
        def _(d):
            attend(tile_of(d, s), [qbuf.at[d, s, c] for c in range(4)], 1 + 2 * s + d)

    def gap_of(tile, keys, k):
        same = jnp.where(offset == positions(tile), 1.0, 0.0)[:, :ROWS].astype(BF16)
        cached = kvb[pl.ds(tile, 1), :, :, :HD].reshape(HD, HD)
        over = (((0,), (0,)), ((), ()))
        found = lax.dot_general(same, cached, over, preferred_element_type=F32)
        hit = lax.dot_general(same, jnp.ones((HD, HD), BF16), over, preferred_element_type=F32)
        gap = (found - keys.astype(F32)) * hit
        squares = (gap * gap).T
        dsend[k, :, :ROWS] = jnp.sum(squares, axis=0, keepdims=True)

    def stats_of(job, h):
        columns = slice(h * 2 * HD, (h + 1) * 2 * HD)
        return pstat[job, 0:1, columns], pstat[job, 1:2, columns]

    def part_of(job, c):
        return part[job, :, c * HD : (c + 1) * HD]

    def combine(d, s, h, job):
        top, total = stats_of(job, h)
        stat_copy(d, s, h).wait_recv()
        other = srecv[d, s, h]
        other_top = jnp.concatenate([other[0:1, :], other[1:2, :]], axis=1)
        other_total = jnp.concatenate([other[2:3, :], other[3:4, :]], axis=1)
        new_top = jnp.maximum(top, other_top)
        mine = jnp.exp2((top - new_top) * LOG2_SCALE)
        theirs = jnp.exp2((other_top - new_top) * LOG2_SCALE)
        return new_top, total * mine + other_total * theirs, mine, theirs

    def summed(d, s, h, i, job, mine, theirs):
        columns = slice(i * HD, (i + 1) * HD)
        out_copy(d, s, 2 * h + i).wait_recv()
        far = orecv[d, s, 2 * h + i].astype(F32)
        return part_of(job, 2 * h + i) * mine[:, columns] + far * theirs[:, columns]

    def hand_on(s, furthest):
        first = s == STEPS - 1 or (s == STEPS - 2 and not furthest)
        factors = []
        for d in range(2):
            h = d if furthest else 1 - d
            job = job_of(d, s)
            if first:
                top, total = stats_of(job, h)
                factors.append(None)
            else:
                top, total, mine, theirs = combine(d, s + 1, h, job)
                factors.append((mine, theirs))
            ssend[d, s, h, 0:1, :] = top[:, :HD]
            ssend[d, s, h, 1:2, :] = top[:, HD:]
            ssend[d, s, h, 2:3, :] = total[:, :HD]
            ssend[d, s, h, 3:4, :] = total[:, HD:]
            stat_copy(d, s, h).start()
        for i in range(2):
            for d in range(2):
                h = d if furthest else 1 - d
                job = job_of(d, s)
                if first:
                    acc = part_of(job, 2 * h + i)
                else:
                    acc = summed(d, s + 1, h, i, job, *factors[d])
                osend[d, s, 2 * h + i] = acc.astype(BF16)
                out_copy(d, s, 2 * h + i).start()

    def gaps(s):
        for d in range(2 if s < STEPS - 1 else 1):
            k = s + 1 if d == 0 else SEQ_BLOCKS // 2 - s - 1
            gap_of(tile_of(d, s), meta[d, s], k)
            dev_copy(k).start()

    dsend[...] = jnp.zeros_like(dsend)
    far_on(2)
    attend(z, [qown.at[c] for c in range(4)], 0)
    near_on(2)
    jobs(2)
    hand_on(2, False)
    for c, d in in_turn(0, 2):
        q_copy(d, 3, c).wait_recv()
    attend(tile_of(0, 3), [qbuf.at[c // 2, 3, c] for c in range(4)], 7)
    hand_on(3, True)
    jobs(1)
    hand_on(1, False)
    meta_copy(0, 3).wait_recv()
    gaps(3)
    gaps(2)
    hand_on(2, True)
    jobs(0)
    hand_on(0, False)
    gaps(1)
    gaps(0)
    gap_of(z, fkv[:, :HD], 0)
    hand_on(1, True)
    for k in range(1, 8):
        dev_copy(k).wait_recv()
    shared = dsend[0]
    for k in range(1, 8):
        shared = shared + drecv[k]
    cbuf[0] = shared
    core_copy().start()

    def outs_left(s):
        for d in range(2):
            for c in range(4):
                if s < STEPS - 1 or c // 2 == d:
                    out_copy(d, s, c).wait_send()
                    if c % 2 == 0:
                        stat_copy(d, s, c // 2).wait_send()

    def half_out(h):
        columns = pl.ds(h * WIDE, WIDE)
        return pltpu.make_async_copy(out_buf.at[:, columns], out_ref.at[:, columns], out_s.at[h])

    next_copy().wait_send()
    for k in range(1, 8):
        rec_copy(k).wait_send()
    for step in range(REQS):
        if step:
            kv_copy(0, step).wait_send()
        kv_copy(1, step).wait_send()
    fresh_copy().wait_send()
    for d in range(2):
        for s in range(STEPS):
            for c in range(4):
                if s < STEPS - 1 or c // 2 == d:
                    q_copy(d, s, c).wait_send()
            if s < STEPS - 1 or d == 0:
                meta_copy(d, s).wait_send()
    for s in (3, 2):
        outs_left(s)
    hand_on(0, True)
    core_copy().wait_recv()
    xbuf[chip] = cbuf[0] + cbuf[1]
    for k in range(1, chips):
        chip_copy(k).start()

    def home(d, h):
        top, total, mine, theirs = combine(d, 0, h, 0)
        columns = slice(h * 2 * HD, (h + 1) * 2 * HD)
        pstat[0, 0:1, columns] = top
        pstat[0, 1:2, columns] = total
        for i in range(2):
            acc = summed(d, 0, h, i, 0, mine, theirs)
            part[0, :, (2 * h + i) * HD : (2 * h + i + 1) * HD] = acc

    for h in range(2):
        home(1 - h, h)
    outs_left(1)
    for k in range(1, chips):
        other = (chip + k) & (chips - 1)
        remote(
            xbuf.at[chip], xbuf.at[other], x_ss.at[k], x_rs.at[other], {"ctx": same_core(k)}
        ).wait_recv()
    gathered = xbuf[0]
    for k in range(1, chips):
        gathered = gathered + xbuf[k]
    dev_ref[...] = gathered[0, :ROWS] / (KVH * HD)

    for h in range(2):
        home(h, h)
        for pair in range(2):
            columns = slice((2 * h + pair) * HD, (2 * h + pair + 1) * HD)
            upright = (part[0, :, columns] / pstat[0, 1:2, columns]).T.astype(BF16)
            for i in range(2):
                head = h * 4 + pair * 2 + i
                out_buf[:, head * HD : (head + 1) * HD] = upright[i * ROWS : (i + 1) * ROWS]
        half_out(h).start()

    outs_left(0)
    for k in range(1, 8):
        dev_copy(k).wait_send()
    core_copy().wait_send()
    for k in range(1, chips):
        chip_copy(k).wait_send()
    for h in range(2):
        half_out(h).wait()


def on_device(fresh_q, fresh_kv, pool_kv, passage_lists, slot_map, rec_pos):
    vmem = pl.BlockSpec(memory_space=pltpu.VMEM)
    anywhere = pl.BlockSpec(memory_space=pl.ANY)
    dma = pltpu.SemaphoreType.DMA
    scratch = [
        pltpu.SMEM(passage_lists.shape, jnp.int32),
        pltpu.SMEM(slot_map.shape, jnp.int32),
        pltpu.VMEM(rec_pos.shape, jnp.int32),
        pltpu.VMEM(fresh_q.shape, BF16),
        pltpu.VMEM(fresh_kv.shape, BF16),
        pltpu.VMEM(pool_kv.shape, BF16),
        pltpu.VMEM((72, HD), F32),
        pltpu.VMEM((REQS, SEQ_BLOCKS, 16, 2 * HD), BF16),
        pltpu.VMEM((SEQ_BLOCKS, 2 * REQS, 16, 2 * HD), BF16),
        pltpu.VMEM((SEQ_BLOCKS // GROUP, HD, GROUP * HD), BF16),
        pltpu.VMEM((SEQ_BLOCKS, HD, HD), jnp.int32),
        pltpu.VMEM((ROWS, 2 * HD), BF16),
        pltpu.VMEM((ROWS, 2 * HD), BF16),
        pltpu.VMEM((HD, HD), BF16),
        pltpu.VMEM((HD, HD), jnp.int32),
        pltpu.VMEM((SEQ_BLOCKS, 2, 1, HD), jnp.int32),
        pltpu.VMEM((4, HD, HD), BF16),
        pltpu.VMEM((2, STEPS, 4, HD, HD), BF16),
        pltpu.VMEM((ROWS, HEADS // KVH * HD), BF16),
        pltpu.VMEM((ROWS, HD), BF16),
        pltpu.VMEM((2, STEPS, ROWS, HD), BF16),
        pltpu.VMEM((GROUP + 1, HD, WIDE), F32),
        pltpu.VMEM((8, HD, WIDE), F32),
        pltpu.VMEM((8, 8, WIDE), F32),
        pltpu.VMEM((2, STEPS, 4, HD, HD), BF16),
        pltpu.VMEM((2, STEPS, 2, 4, HD), F32),
        pltpu.VMEM((2, STEPS, 4, HD, HD), BF16),
        pltpu.VMEM((2, STEPS, 2, 4, HD), F32),
        pltpu.VMEM((8, 1, HD), F32),
        pltpu.VMEM((8, 1, HD), F32),
        pltpu.VMEM((2, 1, HD), F32),
        pltpu.VMEM((CTX // 2, 1, HD), F32),
        pltpu.SemaphoreType.REGULAR,
        pltpu.SemaphoreType.REGULAR,
        pltpu.SemaphoreType.REGULAR,
        dma((2,)),
        dma((7,)),
        dma((2, REQS)), dma((2 * REQS,)),
        dma((SEQ_BLOCKS,)), dma((SEQ_BLOCKS + 1,)),
        dma((1,)), dma((1,)),
        dma((2, STEPS, 4)), dma((2, STEPS, 4)),
        dma((2, STEPS)), dma((2, STEPS)),
        dma((2, STEPS, 4)), dma((2, STEPS, 4)),
        dma((2, STEPS, 2)), dma((2, STEPS, 2)),
        dma((8,)), dma((8,)),
        dma((1,)), dma((1,)),
        dma((CTX // 2,)), dma((CTX // 2,)),
    ]
    output, deviation = pl.pallas_call(
        kernel,
        out_shape=(
            jax.ShapeDtypeStruct((ROWS, HEADS // CTX * HD), BF16),
            jax.ShapeDtypeStruct((ROWS,), F32),
        ),
        in_specs=[anywhere] * 7,
        out_specs=(anywhere, vmem),
        scratch_shapes=scratch,
        compiler_params=pltpu.CompilerParams(
            collective_id=0, has_side_effects=True, vmem_limit_bytes=60 * 2**20
        ),
    )(passage_lists, slot_map, rec_pos, fresh_q, fresh_kv, pool_kv, jnp.asarray(angle_table()))
    return output, deviation


def solution(mesh):
    in_specs = (
        P("pool", "ctx"),
        P("pool", "ctx"),
        P(None, "pool", "ctx"),
        P(),
        P(),
        P("pool", None),
    )
    out_specs = (P("pool", "ctx"), P("pool"))
    return jax.shard_map(
        on_device, mesh=mesh, in_specs=in_specs, out_specs=out_specs, check_vma=False
    )
```
